256 devices in a mesh: group: 8 (over x, core), fsdp: 32 (over z, y).
Axes of the slice: x: 4, y: 4, z: 8, core: 2. Of those that a mesh axis runs over, the one named last changes fastest.
Arguments:
- resid_in: bfloat16 [512, 320, 1536], P(('group', 'fsdp')), may hold values from -44 to 44
- attn_out: bfloat16 [512, 320, 1536], P(('group', 'fsdp')), may hold values from -6 to 6
- target_rows: bfloat16 [512, 320, 1536], P(('group', 'fsdp')), may hold values from -6 to 6
- out_weight: bfloat16 [1536, 1536], P('fsdp'), may hold values from -0.15625 to 0.15625
- norm_gain: bfloat16 [1536], replicated, may hold values from 0.099609375 to 1.8984375
- seq_lengths: int32 [512], replicated, may hold values from 33 to 320, as said below
- prompt_ids: int32 [512], replicated, may hold values from 0 to 63, as said below
- log_offsets: float32 [512], replicated, may hold values from -48 to 57
- plan_dest: int32 [512, 5], replicated, may hold values from -1 to 7, as said below
- plan_slot: int32 [512, 5], replicated, may hold values from -1 to 5, as said below
Outputs:
- resid_grad: bfloat16 [512, 320, 1536], P(('group', 'fsdp'))
- attn_grad: bfloat16 [512, 320, 1536], P(('group', 'fsdp'))
- weight_grad: float32 [1536, 1536], P('fsdp')
- loss: float32 [], replicated
The draws below stay inside these ranges and needn't reach their ends.
Inputs may be any that keep to these rules, and one draw needn't show every extreme that they name: `seq_lengths`: A sequence of length l covers its first ceil(l / 64) buckets; the sequences of one index of fsdp cover exactly 48 buckets together, and on every index of fsdp some device has all 2 sequences of length 320. `plan_dest`: -1 exactly for buckets that the sequence doesn't cover. Among the devices of one index of fsdp, each works on exactly 6 buckets, and no device sends more than 2 of its buckets to one device; some device sends exactly 2 to one device. `plan_slot`: -1 where plan_dest is -1. For one index of fsdp, every pair of working device and position below 6 is taken by exactly one bucket. `prompt_ids`: the sequences of index g along group (g * 2 * 32 onwards) belong to prompts g * 8 to g * 8 + 7, each prompt with exactly 8 sequences.
All inputs are finite; a program needn't handle non-finite values.
Results may differ from the reference program's by a relative error of at most 0.005.
Values may be sent and summed in bfloat16 or wider, within the bound.
A program may use at most 128 MiB of HBM per device.

```python
import math
import jax
import jax.numpy as jnp
from jax import lax

D = 1536
SEQ_DEV = 2
NBLK = 5
BLOCK = 64
PPG = 8
LMAX = 320
SEQS = 512
PROMPTS = 64
SAMPLES = 8
N_GROUP = 8
N_FSDP = 32


def block_plan(key):
    base = jax.random.fold_in(key, 101)
    count = N_GROUP * SEQ_DEV
    pos = jnp.arange(count, dtype=jnp.int32)
    device = pos // SEQ_DEV
    rotate = jax.random.randint(jax.random.fold_in(base, 1), (N_FSDP, 1), 0, N_GROUP)
    relative = (device[None, :] - rotate) % N_GROUP
    forced = relative == 0
    blocks = jnp.where(forced, NBLK, jnp.where((relative == 1) | (relative == 2), 2, 3)).astype(jnp.int32)

    def move(step, blocks):
        step_key = jax.random.fold_in(jax.random.fold_in(base, 2), step)
        pair = jax.random.randint(step_key, (2, N_FSDP, 1), 0, count)
        source = pos[None, :] == pair[0]
        target = pos[None, :] == pair[1]
        source_blocks = jnp.sum(jnp.where(source, blocks, 0), axis=1, keepdims=True)
        target_blocks = jnp.sum(jnp.where(target, blocks, 0), axis=1, keepdims=True)
        source_forced = jnp.any(source & forced, axis=1, keepdims=True)
        target_forced = jnp.any(target & forced, axis=1, keepdims=True)
        accept = ~source_forced & ~target_forced & (pair[0] != pair[1]) & (source_blocks > 1) & (target_blocks < NBLK)
        accept_int = accept.astype(jnp.int32)
        return blocks - accept_int * source.astype(jnp.int32) + accept_int * target.astype(jnp.int32)
    blocks = lax.fori_loop(0, 8 * count, move, blocks)
    trimmed = jax.random.randint(jax.random.fold_in(base, 3), (N_FSDP, count), 0, BLOCK // 2)
    trimmed = jnp.where(forced, 0, trimmed)
    lengths = (blocks * BLOCK - trimmed).astype(jnp.int32)
    covered = (jnp.arange(NBLK, dtype=jnp.int32)[None, None, :] < blocks[:, :, None]).reshape(N_FSDP, count * NBLK)
    order = jnp.cumsum(covered.astype(jnp.int32), axis=1) - 1
    dest = jnp.where(covered, order % N_GROUP, -1).astype(jnp.int32)
    slot = jnp.where(covered, order // N_GROUP, -1).astype(jnp.int32)
    lengths = jnp.transpose(lengths.reshape(N_FSDP, N_GROUP, SEQ_DEV), (1, 0, 2)).reshape(-1)
    dest = jnp.transpose(dest.reshape(N_FSDP, N_GROUP, SEQ_DEV, NBLK), (1, 0, 2, 3)).reshape(-1, NBLK)
    slot = jnp.transpose(slot.reshape(N_FSDP, N_GROUP, SEQ_DEV, NBLK), (1, 0, 2, 3)).reshape(-1, NBLK)
    return (lengths, dest, slot)


def draw_seq_lengths(key, part):
    return block_plan(key)[0]


def draw_plan_dest(key, part):
    return block_plan(key)[1]


def draw_plan_slot(key, part):
    return block_plan(key)[2]


def draw_prompt_ids(key, part):
    keys = jax.random.split(jax.random.fold_in(key, 202), N_GROUP)

    def shuffle_row(row_key):
        return jax.random.permutation(row_key, SEQ_DEV * N_FSDP)
    shuffled = jax.vmap(shuffle_row)(keys)
    ids = jnp.arange(N_GROUP, dtype=jnp.int32)[:, None] * PPG + shuffled % PPG
    return ids.reshape(-1).astype(jnp.int32)


def draw_log_offsets(key, part):
    seq = jnp.arange(SEQS, dtype=jnp.int32)
    column = (seq // SEQ_DEV % N_FSDP).astype(jnp.float32)
    spread = 4.0 + 8.0 * column / max(N_FSDP - 1, 1)
    inner = jax.random.fold_in(key, 303)
    values = jnp.clip(jax.random.normal(inner, (SEQS,), jnp.float32), -4.0, 4.0) * spread
    return values.astype(jnp.float32)


def draw_resid_in(key, part):
    inner = jax.random.fold_in(key, 404)
    values = jnp.clip(jax.random.normal(inner, (SEQS, LMAX, D), jnp.float32), -6.0, 6.0)
    return values.astype(jnp.bfloat16)


def levels(rng, extent, cuts, least, top_value):
    level, own = 1.0, jax.random.fold_in(rng, 6)
    for axis_at, shards_of in cuts:
        steps = jnp.exp(jax.random.uniform(jax.random.fold_in(own, axis_at), (shards_of,), jnp.float32, least / len(cuts), top_value / len(cuts)))
        level = level * jnp.repeat(steps, extent[axis_at] // shards_of).reshape([-1 if axis == axis_at else 1 for axis in range(len(extent))])
    return level


def noise(stream_key, extent, deviation, bound, shards=(), kind=jnp.bfloat16):
    result = deviation * jax.random.normal(stream_key, extent, jnp.float32)
    if shards:
        result = result * levels(stream_key, extent, shards, -0.22, 0.18)
    return jnp.clip(result, -bound, bound).astype(kind)


def setup_inputs(seed: int = 0) -> dict:
    key_list = jax.random.split(jax.random.key(seed), 11)
    return {
        "resid_in": draw_resid_in(jax.random.fold_in(key_list[10], 71), 0),
        "attn_out": noise(key_list[1], (SEQS, LMAX, D), 1.0, 6.0, ((0, 256),)),
        "target_rows": noise(key_list[2], (SEQS, LMAX, D), 1.0, 6.0, ((0, 256),)),
        "out_weight": noise(key_list[3], (D, D), D ** -0.5, 0.15625, ((0, 32),)),
        "norm_gain": jnp.clip(1.0 + 0.18 * jax.random.normal(key_list[4], (D,), jnp.float32), 0.099609375, 1.8984375).astype(jnp.bfloat16),
        "seq_lengths": draw_seq_lengths(jax.random.fold_in(key_list[10], 71), 0),
        "prompt_ids": draw_prompt_ids(jax.random.fold_in(key_list[10], 71), 0),
        "log_offsets": draw_log_offsets(jax.random.fold_in(key_list[10], 71), 0),
        "plan_dest": draw_plan_dest(jax.random.fold_in(key_list[10], 71), 0),
        "plan_slot": draw_plan_slot(jax.random.fold_in(key_list[10], 71), 0),
    }


EPS = 1e-06

def forward_rows(x_rows, o_rows, e_rows, weight, gain, mask):
    width = x_rows.shape[-1]
    mixed = x_rows.astype(jnp.float32) + jnp.dot(o_rows, weight, preferred_element_type=jnp.float32)
    scale_inv = lax.rsqrt(lax.optimization_barrier(jnp.mean(mixed * mixed, axis=-1, keepdims=True)) + EPS)
    normed = mixed * scale_inv * gain.astype(jnp.float32)
    token_logp = lax.optimization_barrier(jnp.sum(normed * e_rows.astype(jnp.float32), axis=-1)) * mask / math.sqrt(width)
    return (mixed, scale_inv, token_logp)

def backward_rows(mixed, scale_inv, e_rows, gain, coeff, weight):
    width = mixed.shape[-1]
    gained = coeff[:, None] * e_rows.astype(jnp.float32) * gain.astype(jnp.float32) / math.sqrt(width)
    inner = lax.optimization_barrier(jnp.mean(mixed * gained, axis=-1, keepdims=True))
    grad_rows = (scale_inv * gained - mixed * scale_inv ** 3 * inner).astype(jnp.bfloat16)
    attn_rows = lax.dot_general(grad_rows, weight, (((1,), (1,)), ((), ())), preferred_element_type=jnp.float32).astype(jnp.bfloat16)
    return (grad_rows, attn_rows)

def reference(resid_in, attn_out, target_rows, out_weight, norm_gain, seq_lengths, prompt_ids, log_offsets, plan_dest, plan_slot):
    positions = jnp.arange(LMAX, dtype=jnp.int32)
    masks = (positions[None, :] < seq_lengths[:, None]).astype(jnp.float32)

    def seq_forward(items):
        x_rows, o_rows, e_rows, mask = items
        mixed, scale_inv, token_logp = forward_rows(x_rows, o_rows, e_rows, out_weight, norm_gain, mask)
        return jnp.sum(token_logp)
    seq_logp = lax.map(seq_forward, (resid_in, attn_out, target_rows, masks))
    delta = seq_logp + log_offsets
    member = (prompt_ids[:, None] == jnp.arange(PROMPTS, dtype=jnp.int32)[None, :]).astype(jnp.float32)
    baseline = lax.optimization_barrier(jnp.sum(member * delta[:, None], axis=0)) / SAMPLES
    centred = delta - lax.optimization_barrier(jnp.sum(member * baseline[None, :], axis=1))
    loss = jnp.sum(centred * centred) / (SEQS * LMAX)

    def seq_backward(total, items):
        x_rows, o_rows, e_rows, mask, weight_seq = items
        mixed, scale_inv, token_logp = forward_rows(x_rows, o_rows, e_rows, out_weight, norm_gain, mask)
        grad_rows, attn_rows = backward_rows(mixed, scale_inv, e_rows, norm_gain, weight_seq * mask, out_weight)
        total = total + lax.dot_general(o_rows, grad_rows, (((0,), (0,)), ((), ())), preferred_element_type=jnp.float32)
        return (total, (grad_rows, attn_rows))
    start = jnp.zeros((D, D), jnp.float32)
    total, outputs = lax.scan(seq_backward, start, (resid_in, attn_out, target_rows, masks, centred))
    return (outputs[0], outputs[1], total / SEQS, loss)
```

```python
import functools
import math

import jax
import jax.numpy as jnp
from jax import lax
from jax.experimental import pallas as pl
from jax.experimental.pallas import tpu as pltpu
from jax.sharding import PartitionSpec as P

MESH = pl.DeviceIdType.MESH
F32, BF16 = jnp.float32, jnp.bfloat16
NX, NC, NZ, NY = 4, 2, 8, 4
EPS = 1e-06
PPG = 8
SAMPLES = 8
D = 1536
TOK = 640
SEQ = 320
H = D // 2
Q = D // 4
RB = 48

Z_ARRIVE = (0, -1, 1, -2, 2, -3, 3, -4)
Y_ARRIVE = (0, -1, 1, -2)
Z_LEAVE = (4, -3, 3, -2, 2, -1, 1, 0)
Y_LEAVE = (2, -1, 1, 0)


class Op:
    def __init__(self, key, waits=(), after=(), sends=(), cost=0.1, rank=0):
        self.key, self.waits, self.after, self.sends, self.cost, self.rank = key, waits, after, sends, cost, rank


def order(ops, size):
    now, done, at, free, out = 0.0, set(), {}, {"z": 0.0, "y": 0.0}, []
    left = list(ops)
    while left:
        best = None
        for n, op in enumerate(left):
            if all(a in done for a in op.after) and all(w in at for w in op.waits):
                ready = max([now] + [at[w] for w in op.waits])
                score = (ready, op.rank, n)
                if best is None or score < best[0]:
                    best = (score, op)
        (ready, _, _), op = best
        left.remove(op)
        now = ready + op.cost
        for axis, event in op.sends:
            start = max(now, free[axis])
            free[axis] = start + size(event)
            at[event] = free[axis] + 1.5
        done.add(op.key)
        out.append(op)
    return out


def gather_ops():
    ops = []

    def a_first(off):
        sends = [("y", ("Ay", "L", 1, off)), ("y", ("Ay", "S", 1, off))]
        if off <= 0 and off > -4:
            sends.insert(0, ("z", ("Az", "L", 1 - off)))
        if off >= 0 and off < 3:
            sends.insert(0, ("z", ("Az", "S", off + 1)))
        return sends

    def b_first(off):
        sends = [("z", ("Bz", "L", 1, off)), ("z", ("Bz", "S", 1, off))]
        if off <= 0 and off > -2:
            sends.insert(0, ("y", ("By", "L", 1 - off)))
        if off == 0:
            sends.insert(0, ("y", ("By", "S", 1)))
        return sends

    ops.append(Op("start", sends=b_first(0) + a_first(0)))
    for off in Z_ARRIVE[1:]:
        event = ("Az", "L" if off < 0 else "S", abs(off))
        ops.append(Op(event, waits=[event], after=["start"], sends=a_first(off)))
    for off in Y_ARRIVE[1:]:
        event = ("By", "L" if off < 0 else "S", abs(off))
        ops.append(Op(event, waits=[event], after=["start"], sends=b_first(off)))
    for off in Z_ARRIVE:
        for d, k, last in (("L", 1, 2), ("L", 2, 2), ("S", 1, 1)):
            event = ("Ay", d, k, off)
            sends = [("y", ("Ay", d, k + 1, off))] if k < last else []
            ops.append(Op(event, waits=[event], after=["start"], sends=sends))
    for off in Y_ARRIVE:
        for d, last in (("L", 4), ("S", 3)):
            for k in range(1, last + 1):
                event = ("Bz", d, k, off)
                sends = [("z", ("Bz", d, k + 1, off))] if k < last else []
                ops.append(Op(event, waits=[event], after=["start"], sends=sends))
    return ops


def scatter_ops():
    ops = []
    for n, yo in enumerate(Y_LEAVE):
        sends = []
        if n == 0:
            sends = [("y", ("Ay", "L", 1, i)) for i in range(8)]
        if n == 1:
            sends = [("y", ("Ay", "S", 1, i)) for i in range(8)]
        ops.append(Op(("CA", n), sends=sends, cost=0.6, rank=2 + n))
    for i, zo in enumerate(Z_LEAVE):
        sends = []
        if i == 0:
            sends = [("z", ("Bz", "L", 1, j)) for j in range(4)]
        if i == 1:
            sends = [("z", ("Bz", "S", 1, j)) for j in range(4)]
        ops.append(Op(("CB", i), sends=sends, cost=0.35, rank=2 + i / 2))
    for i in range(8):
        ops.append(Op(("FA", i), waits=[("Ay", "L", 1, i)], after=[("CA", 0), ("CA", 2)], sends=[("y", ("Ay", "L", 2, i))]))
        waits = [("Ay", "L", 2, i), ("Ay", "S", 1, i)]
        sends = []
        if i >= 2:
            waits.append(("Az", "LS"[i % 2], i // 2) if i < 7 else ("Az", "S", 3))
        if i == 7:
            waits.append(("Az", "L", 4))
        else:
            sends = [("z", ("Az", "LS"[i % 2], i // 2 + 1))]
        ops.append(Op(("TA", i), waits=waits, after=[("CA", 3)], sends=sends))
    for i in range(2, 8):
        for j in range(4):
            if i < 7:
                waits = [("Bz", "LS"[i % 2], i // 2, j)]
                sends = [("z", ("Bz", "LS"[i % 2], i // 2 + 1, j))]
            else:
                waits = [("Bz", "L", 4, j), ("Bz", "S", 3, j)]
                sends = [("y", ("By", "L", 1)), ("y", ("By", "S", 1)), ("y", ("By", "L", 2)), None][j]
                sends = [sends] if sends else []
                if j == 2:
                    waits.append(("By", "L", 1))
                if j == 3:
                    waits += [("By", "L", 2), ("By", "S", 1)]
            ops.append(Op(("FB", i, j), waits=waits, after=[("CB", i)], sends=sends))
    ops.append(Op("loss", after=[("CA", 3), ("CB", 7)], cost=1.0, rank=20))
    for n in range(4):
        ops.append(Op(("attn", n), after=[("CA", 3), ("CB", 7)], cost=1.2, rank=30 + n))
    return ops


GATHER = order(gather_ops(), lambda e: 0.4)
SCATTER = order(scatter_ops(), lambda e: 0.8 if e[0] in ("Az", "By") else 0.4)
G_ID = {e: n for n, e in enumerate(e for op in GATHER for _, e in op.sends)}
S_ID = {e: n for n, e in enumerate(e for op in SCATTER for _, e in op.sends)}


def kernel(
    x_hbm, o_hbm, e_hbm, w_hbm, gain_ref, len_ref, pid_ref, off_ref, prow_ref,
    rg_hbm, ag_hbm, wg_ref, loss_ref,
    wbuf, xb, ob, eb, ot, mixed, ss_ref, t_ref, g, gall, attn,
    da, db, sa, ra, sa2, ra2, sb, rb, sb2, rb2,
    fin, xr, xg, sg, my, mz, msg1, msg2, ls, lx, lmsg1, lmsg2, crow,
    loc, g_send, g_recv, b_send, b_recv, o_send, o_recv, h_send, h_recv, r_send, r_recv,
    y_send, y_recv, z_send, z_recv, x_send, x_recv, w_send, w_recv, c_send, c_recv, l_send, l_recv, m_send, m_recv,
):
    gi, fi = lax.axis_index("group"), lax.axis_index("fsdp")
    x, c = gi // 2, lax.rem(gi, 2)
    z, y = fi // 4, lax.rem(fi, 4)
    s = 1 - 2 * c

    def zat(off):
        return lax.rem(z + off * s + 2 * NZ, NZ)

    def yat(off):
        return lax.rem(y + off * s + 2 * NY, NY)

    def dev(xx, cc, zz, yy):
        return (xx * 2 + cc, zz * 4 + yy)

    peer = {
        ("z", "L"): dev(x, c, zat(1), y),
        ("z", "S"): dev(x, c, zat(-1), y),
        ("y", "L"): dev(x, c, z, yat(1)),
        ("y", "S"): dev(x, c, z, yat(-1)),
    }
    sibling = dev(x, 1 - c, z, y)
    xs = [lax.rem(x + k, NX) for k in range(1, NX)]
    ys = [lax.rem(y + k, NY) for k in range(1, NY)]
    zs = [lax.rem(z + k, NZ) for k in range(1, NZ)]

    def remote(src, dst, send, recv, to):
        return pltpu.make_async_remote_copy(
            src_ref=src, dst_ref=dst, send_sem=send, recv_sem=recv, device_id=to, device_id_type=MESH
        )

    sent = []

    def start(copy):
        copy.start()
        sent.append(copy)

    loads = [
        pltpu.make_async_copy(w_hbm.at[:, 0:H], wbuf.at[0, z, y], loc.at[0]),
        pltpu.make_async_copy(w_hbm.at[:, H:D], wbuf.at[1, z, y], loc.at[1]),
        pltpu.make_async_copy(o_hbm, ob, loc.at[2]),
        pltpu.make_async_copy(x_hbm, xb, loc.at[3]),
        pltpu.make_async_copy(e_hbm, eb, loc.at[4]),
    ]
    for copy in loads:
        copy.start()

    barrier = pltpu.get_barrier_semaphore()
    greet = [sibling]
    greet += [dev(v, c, z, y) for v in xs] + [dev(x, c, z, v) for v in ys] + [dev(x, c, v, y) for v in zs]
    for to in greet:
        pl.semaphore_signal(barrier, inc=1, device_id=to, device_id_type=MESH)
    pl.semaphore_wait(barrier, len(greet))

    loads[0].wait()
    loads[1].wait()

    def block_of(event, sender):
        kind, d, k = event[:3]
        k = k - 1 if sender else k
        step = -k if d == "L" else k
        if kind == "Az":
            zz, yy = zat(step), y
        elif kind == "Ay":
            zz, yy = zat(event[3]), yat(step)
        elif kind == "By":
            zz, yy = z, yat(step)
        else:
            zz, yy = zat(step), yat(event[3])
        cols = pl.ds(0, Q) if kind[0] == "A" else pl.ds(Q, Q)
        return wbuf.at[c, zz, yy, :, cols], wbuf.at[1 - c, zz, yy, :, cols]

    def turn(n):
        piece = ob[:, pl.ds(n * Q, Q)].T
        ot[2 * n : 2 * n + 2, :, :, 0:TOK] = piece.reshape(2, 4, RB, TOK)
        part = ot.at[2 * n : 2 * n + 2, :, :, 0:TOK]
        start(remote(part, ot.at[2 * n : 2 * n + 2, :, :, TOK : 2 * TOK], o_send.at[n], o_recv.at[n], sibling))

    turn_at = {4: 0, 10: 1, 18: 2, 26: 3}
    for step, op in enumerate(GATHER):
        for event in op.waits:
            mine, _ = block_of(event, False)
            remote(mine, mine, g_send.at[G_ID[event]], g_recv.at[G_ID[event]], sibling).wait_recv()
        for axis, event in op.sends:
            blk, _ = block_of(event, True)
            start(remote(blk, blk, g_send.at[G_ID[event]], g_recv.at[G_ID[event]], peer[axis, event[1]]))
        for event in op.waits:
            mine, _ = block_of(event, False)
            start(remote(mine, mine, b_send.at[G_ID[event]], b_recv.at[G_ID[event]], sibling))
        if step == 0:
            loads[2].wait()
        if step in turn_at:
            turn(turn_at[step])
    for event, n in G_ID.items():
        kind, d, k = event[:3]
        step = k if d == "L" else -k
        if kind == "Az":
            zz, yy = zat(step), y
        elif kind == "Ay":
            zz, yy = zat(-event[3]), yat(step)
        elif kind == "By":
            zz, yy = z, yat(step)
        else:
            zz, yy = zat(step), yat(-event[3])
        cols = pl.ds(0, Q) if kind[0] == "A" else pl.ds(Q, Q)
        theirs = wbuf.at[1 - c, zz, yy, :, cols]
        remote(theirs, theirs, b_send.at[n], b_recv.at[n], sibling).wait_recv()
    loads[3].wait()
    loads[4].wait()

    def forward(m, _):
        rows = pl.ds(pl.multiple_of(m * 160, 160), 160)
        ss = jnp.zeros((160, 1), F32)
        tt = jnp.zeros((160, 1), F32)
        for h in range(2):
            cols = pl.ds(h * H, H)
            w = wbuf[h].reshape(D, H)
            acc = jnp.dot(ob[rows, :], w, preferred_element_type=F32) + xb[rows, cols].astype(F32)
            mixed[h, rows, :] = acc
            eg = eb[rows, cols].astype(F32) * gain_ref[:, cols].astype(F32)
            ss = ss + jnp.sum(acc * acc, axis=1, keepdims=True)
            tt = tt + jnp.sum(acc * eg, axis=1, keepdims=True)
        ss_ref[rows, :] = jnp.broadcast_to(ss, (160, 128))
        t_ref[rows, :] = jnp.broadcast_to(tt, (160, 128))
        return 0

    lax.fori_loop(0, TOK // 160, forward, 0)

    first = (gi * 32 + fi) * 2
    lane = lax.broadcasted_iota(jnp.int32, (8, 128), 1)
    pos = lax.broadcasted_iota(jnp.int32, (SEQ, 128), 0)
    root = 1.0 / math.sqrt(D)
    deltas = []
    for j in range(2):
        rows = pl.ds(j * SEQ, SEQ)
        mask = (pos < len_ref[first + j]).astype(F32)
        scale = lax.rsqrt(ss_ref[rows, :] * (1.0 / D) + EPS)
        t = t_ref[rows, :]
        logp = t * scale * mask * root
        deltas.append(jnp.broadcast_to(jnp.sum(logp, axis=0, keepdims=True), (8, 128)) + off_ref[first + j])
        ss_ref[rows, :] = scale * mask * root
        t_ref[rows, :] = -(scale * scale * scale) * mask * (t * (root / D))
    at = lax.rem(gi, 2) * 64 + 2 * fi
    msg1[...] = jnp.where(lane == at, deltas[0], jnp.where(lane == at + 1, deltas[1], 0.0))
    for k in range(3):
        start(remote(msg1, my.at[k], y_send.at[k], y_recv.at[k], dev(x, c, z, ys[k])))
    total = msg1[...]
    for k in range(3):
        remote(my.at[k], my.at[k], y_send.at[k], y_recv.at[k], sibling).wait_recv()
        total = total + my[k]
    msg2[...] = total
    for k in range(7):
        start(remote(msg2, mz.at[k], z_send.at[k], z_recv.at[k], dev(x, c, zs[k], y)))
    for k in range(7):
        remote(mz.at[k], mz.at[k], z_send.at[k], z_recv.at[k], sibling).wait_recv()
        total = total + mz[k]

    prow = jnp.broadcast_to(prow_ref[pl.ds(gi // 2, 1), :], (8, 128))
    for j in range(2):
        base = jnp.sum(jnp.where(prow == pid_ref[first + j], total, 0.0), axis=1, keepdims=True) * (1.0 / SAMPLES)
        crow[j] = deltas[j] - base

    def gradient(m, _):
        rows = pl.ds(pl.multiple_of(m * 64, 64), 64)
        cc = jnp.where(m < 5, crow[0], crow[1])[0:1]
        ga = ss_ref[rows, :] * cc
        gb = t_ref[rows, :] * cc
        ga = jnp.concatenate([ga] * 6, axis=1)
        gb = jnp.concatenate([gb] * 6, axis=1)
        for h in range(2):
            cols = pl.ds(h * H, H)
            eg = eb[rows, cols].astype(F32) * gain_ref[:, cols].astype(F32)
            g[h, rows, :] = (ga * eg + gb * mixed[h, rows, :]).astype(BF16)
        gall[rows, :] = g[c, rows, :]
        return 0

    lax.fori_loop(0, TOK // 64, gradient, 0)
    start(remote(g.at[1 - c], gall.at[pl.ds(TOK, TOK)], h_send.at[0], h_recv.at[0], sibling))
    stores = []
    for h in range(2):
        copy = pltpu.make_async_copy(g.at[h], rg_hbm.at[:, pl.ds(h * H, H)], loc.at[5 + h])
        copy.start()
        stores.append(copy)
    for n in range(4):
        theirs = ot.at[2 * n : 2 * n + 2, :, :, TOK : 2 * TOK]
        remote(theirs, theirs, o_send.at[n], o_recv.at[n], sibling).wait_recv()
    theirs = gall.at[pl.ds(TOK, TOK)]
    remote(theirs, theirs, h_send.at[0], h_recv.at[0], sibling).wait_recv()

    def slot(event):
        kind, d, k = event[:3]
        if kind == "Ay":
            n = (0 if d == "L" else 2) + k - 1
            return sa.at[n, event[3]], ra.at[n, event[3]]
        if kind == "Az":
            n = (0 if d == "L" else 4) + k - 1
            return sa2.at[n], ra2.at[n]
        if kind == "Bz":
            n = (0 if d == "L" else 4) + k - 1
            return sb.at[n, event[3]], rb.at[n, event[3]]
        n = (0 if d == "L" else 2) + k - 1
        return sb2.at[n], rb2.at[n]

    def push(axis, event, value):
        src, dst = slot(event)
        src[...] = value.astype(src.dtype)
        start(remote(src, dst, r_send.at[S_ID[event]], r_recv.at[S_ID[event]], peer[axis, event[1]]))

    for op in SCATTER:
        got = 0.0
        for event in op.waits:
            _, dst = slot(event)
            remote(dst, dst, r_send.at[S_ID[event]], r_recv.at[S_ID[event]], sibling).wait_recv()
            got = got + dst[...].astype(F32)
        kind = op.key[0] if isinstance(op.key, tuple) else op.key
        if kind == "CA":
            yy = yat(Y_LEAVE[op.key[1]])
            lhs = ot[:, yy].reshape(8 * RB, 2 * TOK)
            da[:, yy] = jnp.dot(lhs, gall[:, 0:Q], preferred_element_type=F32).reshape(8, RB, Q)
            for axis, event in op.sends:
                push(axis, event, da[zat(Z_LEAVE[event[3]]), yy])
        elif kind == "CB":
            zz = zat(Z_LEAVE[op.key[1]])
            lhs = ot[zz].reshape(4 * RB, 2 * TOK)
            db[zz] = jnp.dot(lhs, gall[:, Q:H], preferred_element_type=F32).reshape(4, RB, Q)
            for axis, event in op.sends:
                push(axis, event, db[zz, yat(Y_LEAVE[event[3]])])
        elif kind == "FA":
            push(*op.sends[0], da[zat(Z_LEAVE[op.key[1]]), yat(1)] + got)
        elif kind == "TA":
            value = da[zat(Z_LEAVE[op.key[1]]), y] + got
            if op.sends:
                push(*op.sends[0], value)
            else:
                fin[0:2] = value.reshape(2, RB // 2, Q)
        elif kind == "FB":
            value = db[zat(Z_LEAVE[op.key[1]]), yat(Y_LEAVE[op.key[2]])] + got
            if op.sends:
                push(*op.sends[0], value)
            else:
                fin[2:4] = value.reshape(2, RB // 2, Q)
        elif kind == "attn":
            n = op.key[1]
            cols = pl.ds(n * Q, Q)
            w0 = wbuf[0, 2 * n : 2 * n + 2].reshape(Q, H)
            w1 = wbuf[1, 2 * n : 2 * n + 2].reshape(Q, H)
            dims = (((1,), (1,)), ((), ()))
            acc = lax.dot_general(g[0], w0, dims, preferred_element_type=F32)
            acc = acc + lax.dot_general(g[1], w1, dims, preferred_element_type=F32)
            attn[:, cols] = acc.astype(BF16)
            copy = pltpu.make_async_copy(attn.at[:, cols], ag_hbm.at[:, cols], loc.at[7 + n])
            copy.start()
            stores.append(copy)
        else:
            square = jnp.zeros((8, 1), F32)
            for p in range(PPG):
                member = prow == gi * PPG + p
                base = jnp.sum(jnp.where(member, total, 0.0), axis=1, keepdims=True) * (1.0 / SAMPLES)
                off = jnp.where(member, total - base, 0.0)
                square = square + jnp.sum(off * off, axis=1, keepdims=True)
            lmsg1[...] = jnp.broadcast_to(square, (8, 128))
            start(remote(lmsg1, ls, l_send.at[0], l_recv.at[0], sibling))

    for k in range(3):
        start(remote(fin.at[xs[k]], xr.at[k], x_send.at[k], x_recv.at[k], dev(xs[k], c, z, y)))
    remote(ls, ls, l_send.at[0], l_recv.at[0], sibling).wait_recv()
    pair = lmsg1[...] + ls[...]
    lmsg2[...] = pair
    lx[x] = pair
    for k in range(3):
        start(remote(lmsg2, lx.at[x], m_send.at[k], m_recv.at[k], dev(xs[k], c, z, y)))
    value = fin[x]
    for k in range(3):
        remote(xr.at[k], xr.at[k], x_send.at[k], x_recv.at[k], sibling).wait_recv()
        value = value + xr[k]
    xg[c, x] = value * (1.0 / 512.0)
    for k in range(3):
        start(remote(xg.at[c, x], xg.at[c, x], w_send.at[k], w_recv.at[k], dev(xs[k], c, z, y)))
    start(remote(xg.at[c, x], xg.at[c, x], c_send.at[3], c_recv.at[3], sibling))
    for k in range(3):
        src = lax.rem(x + NX - 1 - k, NX)
        blk = xg.at[c, src]
        remote(blk, blk, w_send.at[k], w_recv.at[k], sibling).wait_recv()
        start(remote(blk, blk, c_send.at[k], c_recv.at[k], sibling))
    for k in range(3):
        src = lax.rem(x + NX - 1 - k, NX)
        remote(lx.at[src], lx.at[src], m_send.at[k], m_recv.at[k], sibling).wait_recv()
    whole = (lx[0] + lx[1]) + (lx[2] + lx[3])
    loss_ref[0, 0] = jnp.sum(whole[0:1, 0:1]) * (1.0 / (512 * SEQ))
    for k in range(4):
        src = x if k == 3 else lax.rem(x + NX - 1 - k, NX)
        blk = xg.at[1 - c, src]
        remote(blk, blk, c_send.at[k], c_recv.at[k], sibling).wait_recv()
    for h in range(2):
        for q in range(4):
            rows = pl.ds((q % 2) * 24, 24)
            cols = pl.ds(h * H + (q // 2) * Q, Q)
            wg_ref[rows, cols] = xg[h, q]
    for copy in stores:
        copy.wait()
    for copy in sent:
        copy.wait_send()


def local(
    resid_in, attn_out, target_rows, out_weight, norm_gain,
    seq_lengths, prompt_ids, log_offsets, plan_dest, plan_slot,
):
    hbm = pl.BlockSpec(memory_space=pl.ANY)
    vmem = pl.BlockSpec(memory_space=pltpu.VMEM)
    smem = pl.BlockSpec(memory_space=pltpu.SMEM)
    dma = pltpu.SemaphoreType.DMA
    n_g, n_s = len(G_ID), len(S_ID)
    scratch = [
        pltpu.VMEM((2, NZ, NY, RB, H), BF16),
        pltpu.VMEM((TOK, D), BF16),
        pltpu.VMEM((TOK, D), BF16),
        pltpu.VMEM((TOK, D), BF16),
        pltpu.VMEM((NZ, NY, RB, 2 * TOK), BF16),
        pltpu.VMEM((2, TOK, H), F32),
        pltpu.VMEM((TOK, 128), F32),
        pltpu.VMEM((TOK, 128), F32),
        pltpu.VMEM((2, TOK, H), BF16),
        pltpu.VMEM((2 * TOK, H), BF16),
        pltpu.VMEM((TOK, D), BF16),
        pltpu.VMEM((NZ, NY, RB, Q), F32),
        pltpu.VMEM((NZ, NY, RB, Q), F32),
        pltpu.VMEM((3, 8, RB, Q), BF16),
        pltpu.VMEM((3, 8, RB, Q), BF16),
        pltpu.VMEM((7, RB, Q), F32),
        pltpu.VMEM((7, RB, Q), F32),
        pltpu.VMEM((7, 4, RB, Q), BF16),
        pltpu.VMEM((7, 4, RB, Q), BF16),
        pltpu.VMEM((3, RB, Q), F32),
        pltpu.VMEM((3, RB, Q), F32),
        pltpu.VMEM((4, RB // 2, Q), F32),
        pltpu.VMEM((3, RB // 2, Q), F32),
        pltpu.VMEM((2, 4, RB // 2, Q), F32),
        pltpu.VMEM((RB // 2, Q), F32),
        pltpu.VMEM((3, 8, 128), F32),
        pltpu.VMEM((7, 8, 128), F32),
        pltpu.VMEM((8, 128), F32),
        pltpu.VMEM((8, 128), F32),
        pltpu.VMEM((8, 128), F32),
        pltpu.VMEM((4, 8, 128), F32),
        pltpu.VMEM((8, 128), F32),
        pltpu.VMEM((8, 128), F32),
        pltpu.VMEM((2, 8, 128), F32),
        dma((11,)),
        dma((n_g,)), dma((n_g,)), dma((n_g,)), dma((n_g,)),
        dma((4,)), dma((4,)), dma((1,)), dma((1,)),
        dma((n_s,)), dma((n_s,)),
        dma((3,)), dma((3,)), dma((7,)), dma((7,)),
        dma((3,)), dma((3,)), dma((3,)), dma((3,)), dma((4,)), dma((4,)),
        dma((1,)), dma((1,)), dma((3,)), dma((3,)),
    ]
    call = pl.pallas_call(
        kernel,
        out_shape=(
            jax.ShapeDtypeStruct((TOK, D), BF16),
            jax.ShapeDtypeStruct((TOK, D), BF16),
            jax.ShapeDtypeStruct((RB, D), F32),
            jax.ShapeDtypeStruct((1, 1), F32),
        ),
        in_specs=[hbm, hbm, hbm, hbm, vmem, smem, smem, smem, vmem],
        out_specs=(hbm, hbm, vmem, smem),
        scratch_shapes=scratch,
        name="balance",
        compiler_params=pltpu.CompilerParams(
            collective_id=0, has_side_effects=True, vmem_limit_bytes=60 * 1024 * 1024
        ),
        cost_estimate=pl.CostEstimate(flops=9060000000, bytes_accessed=10000000, transcendentals=640),
    )
    rg, ag, wg, loss = call(
        resid_in.reshape(TOK, D),
        attn_out.reshape(TOK, D),
        target_rows.reshape(TOK, D),
        out_weight,
        norm_gain.reshape(1, D),
        seq_lengths,
        prompt_ids,
        log_offsets,
        prompt_ids.reshape(4, 128),
    )
    return rg.reshape(2, SEQ, D), ag.reshape(2, SEQ, D), wg, loss.reshape(())


def solution(mesh):
    return jax.shard_map(
        local,
        mesh=mesh,
        in_specs=(
            P(("group", "fsdp"), None, None),
            P(("group", "fsdp"), None, None),
            P(("group", "fsdp"), None, None),
            P("fsdp", None),
            P(), P(), P(), P(), P(), P(),
        ),
        out_specs=(
            P(("group", "fsdp"), None, None),
            P(("group", "fsdp"), None, None),
            P("fsdp", None),
            P(),
        ),
        check_vma=False,
    )
```

```python
import functools
import math

import jax
import jax.numpy as jnp
from jax import lax
from jax.experimental import pallas as pl
from jax.experimental.pallas import tpu as pltpu
from jax.sharding import PartitionSpec as P

MESH = pl.DeviceIdType.MESH
F32, BF16 = jnp.float32, jnp.bfloat16
NX, NC, NZ, NY = 4, 2, 8, 4
EPS = 1e-06
PPG = 8
SAMPLES = 8
D = 1536
TOK = 640
SEQ = 320
H = D // 2
Q = D // 4
RB = 48

Z_ARRIVE = (0, -1, 1, -2, 2, -3, 3, -4)
Y_ARRIVE = (0, -1, 1, -2)
Z_LEAVE = (4, -3, 3, -2, 2, -1, 1, 0)
Y_LEAVE = (2, -1, 1, 0)


class Op:
    def __init__(self, key, waits=(), after=(), sends=(), cost=0.1, rank=0):
        self.key, self.waits, self.after, self.sends, self.cost, self.rank = key, waits, after, sends, cost, rank


def order(ops, size):
    now, done, at, free, out = 0.0, set(), {}, {}, []
    left = list(ops)
    while left:
        best = None
        for n, op in enumerate(left):
            if all(a in done for a in op.after) and all(w in at for w in op.waits):
                ready = max([now] + [at[w] for w in op.waits])
                score = (ready, op.rank, n)
                if best is None or score < best[0]:
                    best = (score, op)
        (ready, _, _), op = best
        left.remove(op)
        now = ready + op.cost
        for axis, event in op.sends:
            free[axis] = max(now, free.get(axis, 0.0)) + size(event)
            at[event] = free[axis] + (0.9 if axis == "s" else 2.0 if size(event) > 0.5 else 1.6)
        done.add(op.key)
        out.append(op)
    return out


def hops(event):
    return abs(TO[event[0], event[1]]) if event[0] in ("Az", "By") else 2 if event[1] == "D" else 1


GATHER_TO = {-1: 1, 1: -1, -2: 2, 2: -2, -3: 1, 3: -1, -4: 2}
SCATTER_TO = {4: 2, 3: 1, -3: -1, -2: -2, 2: 2, -1: -1, 1: 1}
TO = {}


def gather_ops():
    ops = []
    TO.clear()
    TO.update({("Az", n): v for n, v in GATHER_TO.items()})
    TO.update({("By", n): GATHER_TO[n] for n in (-1, 1, -2)})

    def a_first(off):
        sends = [("y", ("Ay", "L", 1, off)), ("y", ("Ay", "S", 1, off))]
        if off in LATE:
            sends.append(("y", ("Ay", "D", 2, off)))
        if off == 0:
            sends = [("z", ("Az", n)) for n in (-2, 2, -1, 1)] + sends
        if off == -2:
            sends = [("z", ("Az", -4)), ("z", ("Az", -3))] + sends
        if off == 2:
            sends = [("z", ("Az", 3))] + sends
        return sends

    def b_first(off):
        sends = [("z", ("Bz", "L", 1, off)), ("z", ("Bz", "S", 1, off))]
        if off == 0:
            sends = [("y", ("By", n)) for n in (-2, -1, 1)] + sends
        return sends

    ops.append(Op("start", sends=a_first(0)[:4] + b_first(0) + a_first(0)[4:]))
    for off in Z_ARRIVE[1:]:
        ops.append(Op(("Az", off), waits=[("Az", off)], after=["start"], sends=a_first(off)))
    for off in Y_ARRIVE[1:]:
        ops.append(Op(("By", off), waits=[("By", off)], after=["start"], sends=b_first(off)))
    for off in Z_ARRIVE:
        for d, k in (("L", 1), ("D", 2) if off in LATE else ("L", 2), ("S", 1)):
            event = ("Ay", d, k, off)
            sends = [("y", ("Ay", d, k + 1, off))] if k == 1 and d == "L" and off not in LATE else []
            ops.append(Op(event, waits=[event], after=["start"], sends=sends))
    for off in Y_ARRIVE:
        for d, last in (("L", 4), ("S", 3)):
            for k in range(1, last + 1):
                event = ("Bz", d, k, off)
                sends = [("z", ("Bz", d, k + 1, off))] if k < last else []
                ops.append(Op(event, waits=[event], after=["start"], sends=sends))
    return ops


LATE = (-3, 3, -4)


def scatter_ops():
    ops = []
    TO.clear()
    TO.update({("Az", n): v for n, v in SCATTER_TO.items()})
    TO.update({("By", n): SCATTER_TO[n] for n in (2, -1, 1)})
    for n, yo in enumerate(Y_LEAVE):
        sends = []
        if n == 0:
            sends = [("y", ("Ay", "L", 1, i)) for i in range(8)]
        if n == 1:
            sends = [("y", ("Ay", "S", 1, i)) for i in range(8)]
        ops.append(Op(("CA", n), sends=sends, cost=0.6, rank=2 + n))
    for i, zo in enumerate(Z_LEAVE):
        sends = []
        if i == 0:
            sends = [("z", ("Bz", "L", 1, j)) for j in range(4)]
        if i == 1:
            sends = [("z", ("Bz", "S", 1, j)) for j in range(4)]
        ops.append(Op(("CB", i), sends=sends, cost=0.35, rank=2 + i / 2))
    for i, off in enumerate(Z_LEAVE):
        ops.append(Op(("FA", i), waits=[("Ay", "L", 1, i)], after=[("CA", 0), ("CA", 2)], sends=[("y", ("Ay", "L", 2, i))]))
        waits = [("Ay", "L", 2, i), ("Ay", "S", 1, i)]
        waits += [("Az", n) for n in {2: (4, 3), -2: (-3,), 0: (2, -2, 1, -1)}.get(off, ())]
        sends = [("z", ("Az", off))] if off else [("x", ("X", 0, k)) for k in range(3)]
        ops.append(Op(("TA", i), waits=waits, after=[("CA", 3)], sends=sends))
    for i in range(2, 8):
        for j, off in enumerate(Y_LEAVE):
            if i < 7:
                waits = [("Bz", "LS"[i % 2], i // 2, j)]
                sends = [("z", ("Bz", "LS"[i % 2], i // 2 + 1, j))]
            else:
                waits = [("Bz", "L", 4, j), ("Bz", "S", 3, j)]
                sends = [("y", ("By", off))]
                if off == 0:
                    waits += [("By", 2), ("By", -1), ("By", 1)]
                    sends = [("x", ("X", 1, k)) for k in range(3)]
            ops.append(Op(("FB", i, j), waits=waits, after=[("CB", i)], sends=sends))
    for ab in range(2):
        ops.append(Op(("X", ab), waits=[("X", ab, k) for k in range(3)], sends=[("s", ("G", ab))]))
    for ab in range(2):
        ops.append(Op(("W", ab), waits=[("G", ab)]))
    ops.append(Op("loss", after=[("CA", 3), ("CB", 7)], cost=1.0, rank=20, sends=[("s", ("l1",))]))
    ops.append(Op("pair", waits=[("l1",)], sends=[("x", ("l2", k)) for k in range(3)]))
    ops.append(Op("total", waits=[("l2", k) for k in range(3)]))
    for n in range(4):
        ops.append(Op(("attn", n), after=[("CA", 3), ("CB", 7)], cost=1.2, rank=30 + n))
    return ops


def size(event):
    if event[0] in ("l1", "l2"):
        return 0.05
    if event[0] == "X":
        return 1.1
    if event[0] == "G":
        return 0.15
    return 0.4 * hops(event)


GATHER = order(gather_ops(), size)
SCATTER = order(scatter_ops(), size)
G_ID = {e: n for n, e in enumerate(e for op in GATHER for _, e in op.sends)}
S_ID = {e: n for n, e in enumerate(e for op in SCATTER for _, e in op.sends)}


def kernel(
    x_hbm, o_hbm, e_hbm, w_hbm, gain_hbm, len_hbm, pid_hbm, off_hbm, prow_hbm,
    rg_out, ag_out, wg_ref, loss_ref,
    wbuf, xb, ob, eb, ot, mixed, ss_ref, t_ref, g, gall,
    da, db, sa, ra, sa2, ra2, sb, rb, sb2, rb2,
    xr, xg, my, mz, msg1, msg2, ls, lx, lmsg1, lmsg2, crow,
    gain_in, gain_ref, len_ref, pid_ref, off_ref, prow_ref, gauge,
    loc, g_send, g_recv, b_send, b_recv, o_send, o_recv, h_send, h_recv, r_recv,
    a_send, a2_send, s_send, s2_send, x_send, q_send, y_send, y_recv, z_send, z_recv, l_send, m_send,
):
    gi, fi = lax.axis_index("group"), lax.axis_index("fsdp")
    x, c = gi // 2, lax.rem(gi, 2)
    z, y = fi // 4, lax.rem(fi, 4)
    s = 1 - 2 * c

    z_off = {off: lax.rem(z + off * s + 2 * NZ, NZ) for off in range(-4, 5)}
    y_off = {off: lax.rem(y + off * s + 2 * NY, NY) for off in range(-2, 3)}
    zat, yat = z_off.get, y_off.get

    def dev(xx, cc, zz, yy):
        return (xx * 2 + cc, zz * 4 + yy)

    def peer(event, to):
        kind, d = event[:2]
        if kind in ("Az", "By"):
            return dev(x, c, zat(to[d]), y) if kind == "Az" else dev(x, c, z, yat(to[d]))
        step = {"L": 1, "S": -1, "D": 2}[d]
        return dev(x, c, zat(step), y) if kind == "Bz" else dev(x, c, z, yat(step))

    sibling = dev(x, 1 - c, z, y)
    xs = [lax.rem(x + k, NX) for k in range(1, NX)]
    ys = [lax.rem(y + k, NY) for k in range(1, NY)]
    zs = [lax.rem(z + k, NZ) for k in range(1, NZ)]

    def remote(src, dst, send, recv, to):
        return pltpu.make_async_remote_copy(
            src_ref=src, dst_ref=dst, send_sem=send, recv_sem=recv, device_id=to, device_id_type=MESH
        )

    sent = []

    def start(copy):
        copy.start()
        sent.append(copy)

    loads = [
        pltpu.make_async_copy(w_hbm.at[:, 0:H], wbuf.at[0, z, y], loc.at[0]),
        pltpu.make_async_copy(w_hbm.at[:, H:D], wbuf.at[1, z, y], loc.at[1]),
        pltpu.make_async_copy(o_hbm, ob, loc.at[2]),
        pltpu.make_async_copy(x_hbm, xb, loc.at[3]),
        pltpu.make_async_copy(e_hbm, eb, loc.at[4]),
        pltpu.make_async_copy(gain_hbm, gain_in, loc.at[5]),
        pltpu.make_async_copy(len_hbm, len_ref, loc.at[6]),
        pltpu.make_async_copy(pid_hbm, pid_ref, loc.at[7]),
        pltpu.make_async_copy(off_hbm, off_ref, loc.at[8]),
        pltpu.make_async_copy(prow_hbm, prow_ref, loc.at[9]),
    ]
    for copy in loads:
        copy.start()

    barrier = pltpu.get_barrier_semaphore()
    greet = [sibling]
    greet += [dev(v, c, z, y) for v in xs] + [dev(x, c, z, v) for v in ys] + [dev(x, c, v, y) for v in zs]
    for to in greet:
        pl.semaphore_signal(barrier, inc=1, device_id=to, device_id_type=MESH)
    pl.semaphore_wait(barrier, len(greet))

    loads[0].wait()
    loads[1].wait()

    def block_of(event, sender):
        kind = event[0]
        if kind in ("Az", "By"):
            step = event[1]
            if sender:
                step += GATHER_TO[step]
            zz, yy = (zat(step), y) if kind == "Az" else (z, yat(step))
        else:
            d, k, off = event[1:]
            k = (0 if d == "D" else k - 1) if sender else k
            step = k if d == "S" else -k
            zz, yy = (zat(off), yat(step)) if kind == "Ay" else (zat(step), yat(off))
        cols = pl.ds(0, Q) if kind[0] == "A" else pl.ds(Q, Q)
        return wbuf.at[c, zz, yy, :, cols]

    def turn(n):
        piece = ob[:, pl.ds(n * Q, Q)].T
        ot[2 * n : 2 * n + 2, :, :, 0:TOK] = piece.reshape(2, 4, RB, TOK)
        part = ot.at[2 * n : 2 * n + 2, :, :, 0:TOK]
        start(remote(part, ot.at[2 * n : 2 * n + 2, :, :, TOK : 2 * TOK], o_send.at[n], o_recv.at[n], sibling))

    turn_at = {4: 0, 10: 1, 18: 2, 26: 3}
    for step, op in enumerate(GATHER):
        for event in op.waits:
            mine = block_of(event, False)
            remote(mine, mine, g_send.at[0], g_recv.at[G_ID[event]], sibling).wait_recv()
        for axis, event in op.sends:
            part = 0 if event[0][0] == "A" else 1
            blk = block_of(event, True)
            remote(blk, blk, g_send.at[part], g_recv.at[G_ID[event]], peer(event, GATHER_TO)).start()
        for event in op.waits:
            part = 0 if event[0][0] == "A" else 1
            mine = block_of(event, False)
            remote(mine, mine, b_send.at[part], b_recv.at[part], sibling).start()
        if step == 0:
            loads[2].wait()
        if step in turn_at:
            turn(turn_at[step])
    for part in range(2):
        remote(gauge, gauge, b_send.at[part], b_recv.at[part], sibling).wait_recv()
    for copy in loads[3:]:
        copy.wait()
    wide = gain_in[...].astype(F32)
    gain_ref[...] = jnp.concatenate([wide[n : n + 1] for n in range(D // 128)], axis=1)

    def forward(m, _):
        rows = pl.ds(pl.multiple_of(m * 160, 160), 160)
        ss = jnp.zeros((160, 1), F32)
        tt = jnp.zeros((160, 1), F32)
        for h in range(2):
            cols = pl.ds(h * H, H)
            w = wbuf[h].reshape(D, H)
            acc = jnp.dot(ob[rows, :], w, preferred_element_type=F32) + xb[rows, cols].astype(F32)
            mixed[h, rows, :] = acc
            eg = eb[rows, cols].astype(F32) * gain_ref[:, cols]
            ss = ss + jnp.sum(acc * acc, axis=1, keepdims=True)
            tt = tt + jnp.sum(acc * eg, axis=1, keepdims=True)
        ss_ref[rows, :] = jnp.broadcast_to(ss, (160, 128))
        t_ref[rows, :] = jnp.broadcast_to(tt, (160, 128))
        return 0

    lax.fori_loop(0, TOK // 160, forward, 0)

    first = (gi * 32 + fi) * 2
    lane = lax.broadcasted_iota(jnp.int32, (8, 128), 1)
    pos = lax.broadcasted_iota(jnp.int32, (SEQ, 128), 0)
    root = 1.0 / math.sqrt(D)
    deltas = []
    for j in range(2):
        rows = pl.ds(j * SEQ, SEQ)
        mask = (pos < len_ref[first + j]).astype(F32)
        scale = lax.rsqrt(ss_ref[rows, :] * (1.0 / D) + EPS)
        t = t_ref[rows, :]
        logp = t * scale * mask * root
        deltas.append(jnp.broadcast_to(jnp.sum(logp, axis=0, keepdims=True), (8, 128)) + off_ref[first + j])
        ss_ref[rows, :] = scale * mask * root
        t_ref[rows, :] = -(scale * scale * scale) * mask * (t * (root / D))
    at = lax.rem(gi, 2) * 64 + 2 * fi
    msg1[...] = jnp.where(lane == at, deltas[0], jnp.where(lane == at + 1, deltas[1], 0.0))

    def prepare(m, _):
        rows = pl.ds(pl.multiple_of(m * 64, 64), 64)
        ga = jnp.concatenate([ss_ref[rows, :]] * 6, axis=1)
        gb = jnp.concatenate([t_ref[rows, :]] * 6, axis=1)
        for h in range(2):
            cols = pl.ds(h * H, H)
            eg = eb[rows, cols].astype(F32) * gain_ref[:, cols]
            mixed[h, rows, :] = ga * eg + gb * mixed[h, rows, :]
        return 0

    for k in range(3):
        start(remote(msg1, my.at[k], y_send.at[k], y_recv.at[k], dev(x, c, z, ys[k])))
    lax.fori_loop(0, 4, prepare, 0)
    total = msg1[...]
    for k in range(3):
        remote(my.at[k], my.at[k], y_send.at[k], y_recv.at[k], sibling).wait_recv()
        total = total + my[k]
    msg2[...] = total
    for k in range(7):
        start(remote(msg2, mz.at[k], z_send.at[k], z_recv.at[k], dev(x, c, zs[k], y)))
    lax.fori_loop(4, 10, prepare, 0)
    for part in range(2):
        remote(gauge, gauge, g_send.at[part], g_recv.at[0], sibling).wait_send()
        remote(gauge, gauge, b_send.at[part], g_recv.at[0], sibling).wait_send()
    for k in range(7):
        remote(mz.at[k], mz.at[k], z_send.at[k], z_recv.at[k], sibling).wait_recv()
        total = total + mz[k]

    prow = jnp.broadcast_to(prow_ref[pl.ds(gi // 2, 1), :], (8, 128))
    for j in range(2):
        base = jnp.sum(jnp.where(prow == pid_ref[first + j], total, 0.0), axis=1, keepdims=True) * (1.0 / SAMPLES)
        crow[j] = deltas[j] - base

    def gradient(m, _):
        rows = pl.ds(pl.multiple_of(m * 64, 64), 64)
        cc = jnp.where(m < 5, crow[0], crow[1])[0:1]
        cc = jnp.concatenate([cc] * 6, axis=1)
        for h in range(2):
            value = (mixed[h, rows, :] * cc).astype(BF16)
            g[h, rows, :] = value
            rg_out[rows, h * H : (h + 1) * H] = value
        gall[rows, :] = g[c, rows, :]
        return 0

    lax.fori_loop(0, TOK // 64, gradient, 0)
    start(remote(g.at[1 - c], gall.at[pl.ds(TOK, TOK)], h_send.at[0], h_recv.at[0], sibling))
    for n in range(4):
        theirs = ot.at[2 * n : 2 * n + 2, :, :, TOK : 2 * TOK]
        remote(theirs, theirs, o_send.at[n], o_recv.at[n], sibling).wait_recv()
    theirs = gall.at[pl.ds(TOK, TOK)]
    remote(theirs, theirs, h_send.at[0], h_recv.at[0], sibling).wait_recv()

    def slot(event):
        kind, d = event[:2]
        if kind == "Ay":
            n = (0 if d == "L" else 2) + event[2] - 1
            return sa.at[n, event[3]], ra.at[n, event[3]], a_send
        if kind == "Az":
            n = list(SCATTER_TO).index(d)
            return sa2.at[n], ra2.at[n], a2_send
        if kind == "Bz":
            n = (0 if d == "L" else 4) + event[2] - 1
            return sb.at[n, event[3]], rb.at[n, event[3]], s_send
        n = (2, -1, 1).index(d)
        return sb2.at[n], rb2.at[n], s2_send

    def push(event, value):
        src, dst, sem = slot(event)
        src[...] = value.astype(BF16)
        remote(src, dst, sem.at[0], r_recv.at[S_ID[event]], peer(event, SCATTER_TO)).start()

    def got_of(event):
        if event[0] == "X":
            return xr.at[event[1], lax.rem(x + NX - 1 - event[2], NX)]
        if event[0] == "G":
            return xg.at[1 - c, event[1]]
        if event[0] == "l1":
            return ls
        if event[0] == "l2":
            return lx.at[lax.rem(x + NX - 1 - event[1], NX)]
        return slot(event)[1]

    def spread(ab, value):
        xr[ab, x] = value
        for k in range(3):
            blk = xr.at[ab, x]
            remote(blk, blk, x_send.at[ab], r_recv.at[S_ID["X", ab, k]], dev(xs[k], c, z, y)).start()

    for op in SCATTER:
        got = 0.0
        for event in op.waits:
            dst = got_of(event)
            remote(dst, dst, a_send.at[0], r_recv.at[S_ID[event]], sibling).wait_recv()
            if event[0] in ("Ay", "Az", "By", "Bz"):
                got = got + dst[...].astype(F32)
        kind = op.key[0] if isinstance(op.key, tuple) else op.key
        if kind == "CA":
            yy = yat(Y_LEAVE[op.key[1]])
            lhs = ot[:, yy].reshape(8 * RB, 2 * TOK)
            da[:, yy] = jnp.dot(lhs, gall[:, 0:Q], preferred_element_type=F32).reshape(8, RB, Q)
            for axis, event in op.sends:
                push(event, da[zat(Z_LEAVE[event[3]]), yy])
        elif kind == "CB":
            zz = zat(Z_LEAVE[op.key[1]])
            lhs = ot[zz].reshape(4 * RB, 2 * TOK)
            db[zz] = jnp.dot(lhs, gall[:, Q:H], preferred_element_type=F32).reshape(4, RB, Q)
            for axis, event in op.sends:
                push(event, db[zz, yat(Y_LEAVE[event[3]])])
        elif kind == "FA":
            push(op.sends[0][1], da[zat(Z_LEAVE[op.key[1]]), yat(1)] + got)
        elif kind == "TA":
            value = da[zat(Z_LEAVE[op.key[1]]), y] + got
            if Z_LEAVE[op.key[1]]:
                push(op.sends[0][1], value)
            else:
                spread(0, value)
        elif kind == "FB":
            value = db[zat(Z_LEAVE[op.key[1]]), yat(Y_LEAVE[op.key[2]])] + got
            if op.sends[0][0] != "x":
                push(op.sends[0][1], value)
            else:
                spread(1, value)
        elif kind == "X":
            ab = op.key[1]
            value = ((xr[ab, 0] + xr[ab, 1]) + (xr[ab, 2] + xr[ab, 3])) * (1.0 / 512.0)
            xg[c, ab] = value
            blk = xg.at[c, ab]
            start(remote(blk, blk, q_send.at[ab], r_recv.at[S_ID["G", ab]], sibling))
        elif kind == "W":
            ab = op.key[1]
            for h in range(2):
                wg_ref[:, pl.ds(h * H + ab * Q, Q)] = xg[h, ab]
        elif kind == "pair":
            pair = lmsg1[...] + ls[...]
            lmsg2[...] = pair
            lx[x] = pair
            for k in range(3):
                start(remote(lmsg2, lx.at[x], m_send.at[k], r_recv.at[S_ID["l2", k]], dev(xs[k], c, z, y)))
        elif kind == "total":
            whole = (lx[0] + lx[1]) + (lx[2] + lx[3])
            loss_ref[0, 0] = jnp.sum(whole[0:1, 0:1]) * (1.0 / (512 * SEQ))
        elif kind == "attn":
            n = op.key[1]
            cols = pl.ds(n * Q, Q)
            w0 = wbuf[0, 2 * n : 2 * n + 2].reshape(Q, H)
            w1 = wbuf[1, 2 * n : 2 * n + 2].reshape(Q, H)
            dims = (((1,), (1,)), ((), ()))
            acc = lax.dot_general(g[0], w0, dims, preferred_element_type=F32)
            acc = acc + lax.dot_general(g[1], w1, dims, preferred_element_type=F32)
            ag_out[:, cols] = acc.astype(BF16)
        else:
            square = jnp.zeros((8, 1), F32)
            for p in range(PPG):
                member = prow == gi * PPG + p
                base = jnp.sum(jnp.where(member, total, 0.0), axis=1, keepdims=True) * (1.0 / SAMPLES)
                off = jnp.where(member, total - base, 0.0)
                square = square + jnp.sum(off * off, axis=1, keepdims=True)
            lmsg1[...] = jnp.broadcast_to(square, (8, 128))
            start(remote(lmsg1, ls, l_send.at[0], r_recv.at[S_ID[("l1",)]], sibling))

    for ref, sem in ((sa, a_send), (sa2, a2_send), (sb, s_send), (sb2, s2_send)):
        remote(ref, ref, sem.at[0], r_recv.at[0], sibling).wait_send()
    for ab in range(2):
        ref = xr.at[ab, 0:3]
        remote(ref, ref, x_send.at[ab], r_recv.at[0], sibling).wait_send()
    for copy in sent:
        copy.wait_send()


def local(
    resid_in, attn_out, target_rows, out_weight, norm_gain,
    seq_lengths, prompt_ids, log_offsets, plan_dest, plan_slot,
):
    hbm = pl.BlockSpec(memory_space=pl.ANY)
    vmem = pl.BlockSpec(memory_space=pltpu.VMEM)
    smem = pl.BlockSpec(memory_space=pltpu.SMEM)
    dma = pltpu.SemaphoreType.DMA
    n_g, n_s = len(G_ID), len(S_ID)
    scratch = [
        pltpu.VMEM((2, NZ, NY, RB, H), BF16),
        pltpu.VMEM((TOK, D), BF16),
        pltpu.VMEM((TOK, D), BF16),
        pltpu.VMEM((TOK, D), BF16),
        pltpu.VMEM((NZ, NY, RB, 2 * TOK), BF16),
        pltpu.VMEM((2, TOK, H), F32),
        pltpu.VMEM((TOK, 128), F32),
        pltpu.VMEM((TOK, 128), F32),
        pltpu.VMEM((2, TOK, H), BF16),
        pltpu.VMEM((2 * TOK, H), BF16),
        pltpu.VMEM((NZ, NY, RB, Q), F32),
        pltpu.VMEM((NZ, NY, RB, Q), F32),
        pltpu.VMEM((3, 8, RB, Q), BF16),
        pltpu.VMEM((3, 8, RB, Q), BF16),
        pltpu.VMEM((7, RB, Q), BF16),
        pltpu.VMEM((7, RB, Q), BF16),
        pltpu.VMEM((7, 4, RB, Q), BF16),
        pltpu.VMEM((7, 4, RB, Q), BF16),
        pltpu.VMEM((3, RB, Q), BF16),
        pltpu.VMEM((3, RB, Q), BF16),
        pltpu.VMEM((2, 4, RB, Q), F32),
        pltpu.VMEM((2, 2, RB, Q), F32),
        pltpu.VMEM((3, 8, 128), F32),
        pltpu.VMEM((7, 8, 128), F32),
        pltpu.VMEM((8, 128), F32),
        pltpu.VMEM((8, 128), F32),
        pltpu.VMEM((8, 128), F32),
        pltpu.VMEM((4, 8, 128), F32),
        pltpu.VMEM((8, 128), F32),
        pltpu.VMEM((8, 128), F32),
        pltpu.VMEM((2, 8, 128), F32),
        pltpu.VMEM((D // 128, 128), BF16),
        pltpu.VMEM((1, D), F32),
        pltpu.SMEM((512,), jnp.int32),
        pltpu.SMEM((512,), jnp.int32),
        pltpu.SMEM((512,), F32),
        pltpu.VMEM((4, 128), jnp.int32),
        pltpu.VMEM((31, RB, Q), BF16),
        dma((10,)),
        dma((2,)), dma((n_g,)), dma((2,)), dma((2,)),
        dma((4,)), dma((4,)), dma((1,)), dma((1,)),
        dma((n_s,)),
        dma((1,)), dma((1,)), dma((1,)), dma((1,)), dma((2,)), dma((2,)),
        dma((3,)), dma((3,)), dma((7,)), dma((7,)),
        dma((1,)), dma((3,)),
    ]
    call = pl.pallas_call(
        kernel,
        out_shape=(
            pltpu.VMEM((TOK, D), BF16),
            pltpu.VMEM((TOK, D), BF16),
            pltpu.VMEM((RB, D), F32),
            jax.ShapeDtypeStruct((1, 1), F32),
        ),
        in_specs=[hbm] * 9,
        out_specs=(vmem, vmem, vmem, smem),
        scratch_shapes=scratch,
        name="balance",
        compiler_params=pltpu.CompilerParams(
            collective_id=0, has_side_effects=True, vmem_limit_bytes=48 * 1024 * 1024
        ),
        cost_estimate=pl.CostEstimate(flops=9060000000, bytes_accessed=10000000, transcendentals=640),
    )
    operands = (
        resid_in.reshape(TOK, D),
        attn_out.reshape(TOK, D),
        target_rows.reshape(TOK, D),
        out_weight,
        norm_gain.reshape(D // 128, 128),
        seq_lengths,
        prompt_ids,
        log_offsets,
        prompt_ids.reshape(4, 128),
    )
    rg, ag, wg, loss = call(*(pltpu.with_memory_space_constraint(v, pltpu.HBM) for v in operands))
    return rg.reshape(2, SEQ, D), ag.reshape(2, SEQ, D), wg, loss.reshape(())


def solution(mesh):
    return jax.shard_map(
        local,
        mesh=mesh,
        in_specs=(
            P(("group", "fsdp"), None, None),
            P(("group", "fsdp"), None, None),
            P(("group", "fsdp"), None, None),
            P("fsdp", None),
            P(), P(), P(), P(), P(), P(),
        ),
        out_specs=(
            P(("group", "fsdp"), None, None),
            P(("group", "fsdp"), None, None),
            P("fsdp", None),
            P(),
        ),
        check_vma=False,
    )
```

```python
import functools
import math

import jax
import jax.numpy as jnp
from jax import lax
from jax.experimental import pallas as pl
from jax.experimental.pallas import tpu as pltpu
from jax.sharding import PartitionSpec as P

MESH = pl.DeviceIdType.MESH
F32, BF16 = jnp.float32, jnp.bfloat16
NX, NC, NZ, NY = 4, 2, 8, 4
EPS = 1e-06
PPG = 8
SAMPLES = 8
D = 1536
TOK = 640
SEQ = 320
H = D // 2
Q = D // 4
QA, QB = 512, 256
RB = 48

Z_ARRIVE = (0, -1, 1, -2, 2, -3, 3, -4)
Y_ARRIVE = (0, -1, 1, -2)
Z_LEAVE = (4, -3, 3, -2, 2, -1, 1, 0)
Y_LEAVE = (2, -1, 1, 0)


class Op:
    def __init__(self, key, waits=(), after=(), sends=(), cost=0.1, rank=0):
        self.key, self.waits, self.after, self.sends, self.cost, self.rank = key, waits, after, sends, cost, rank


def order(ops, size):
    now, done, at, free, out = 0.0, set(), {}, {}, []
    left = list(ops)
    while left:
        best = None
        for n, op in enumerate(left):
            if all(a in done for a in op.after) and all(w in at for w in op.waits):
                ready = max([now] + [at[w] for w in op.waits])
                score = (ready, op.rank, n)
                if best is None or score < best[0]:
                    best = (score, op)
        (ready, _, _), op = best
        left.remove(op)
        now = ready + op.cost
        for axis, event in op.sends:
            free[axis] = max(now, free.get(axis, 0.0)) + size(event)
            at[event] = free[axis] + (0.9 if axis == "s" else 2.0 if size(event) > 0.5 else 1.6)
        done.add(op.key)
        out.append(op)
    return out


def hops(event):
    return abs(TO[event[0], event[1]]) if event[0] in ("Az", "By") else 2 if event[1] == "D" else 1


GATHER_TO = {-1: 1, 1: -1, -2: 2, 2: -2, -3: 1, 3: -1, -4: 2}
SCATTER_TO = {4: 2, 3: 1, -3: -1, -2: -2, 2: 2, -1: -1, 1: 1}
TO = {}


def gather_ops():
    ops = []
    TO.clear()
    TO.update({("Az", n): v for n, v in GATHER_TO.items()})
    TO.update({("By", n): GATHER_TO[n] for n in (-1, 1, -2)})

    def a_first(off):
        sends = [("y", ("Ay", "L", 1, off)), ("y", ("Ay", "S", 1, off))]
        if off in LATE:
            sends.append(("y", ("Ay", "D", 2, off)))
        if off == 0:
            sends = [("z", ("Az", n)) for n in (-2, 2, -1, 1)] + sends
        if off == -2:
            sends = [("z", ("Az", -4)), ("z", ("Az", -3))] + sends
        if off == 2:
            sends = [("z", ("Az", 3))] + sends
        return sends

    def b_first(off):
        sends = [("z", ("Bz", "L", 1, off)), ("z", ("Bz", "S", 1, off))]
        if off == 0:
            sends = [("y", ("By", n)) for n in (-2, -1, 1)] + sends
        return sends

    ops.append(Op("start", sends=a_first(0)[:4] + b_first(0) + a_first(0)[4:]))
    for off in Z_ARRIVE[1:]:
        ops.append(Op(("Az", off), waits=[("Az", off)], after=["start"], sends=a_first(off)))
    for off in Y_ARRIVE[1:]:
        ops.append(Op(("By", off), waits=[("By", off)], after=["start"], sends=b_first(off)))
    for off in Z_ARRIVE:
        for d, k in (("L", 1), ("D", 2) if off in LATE else ("L", 2), ("S", 1)):
            event = ("Ay", d, k, off)
            sends = [("y", ("Ay", d, k + 1, off))] if k == 1 and d == "L" and off not in LATE else []
            ops.append(Op(event, waits=[event], after=["start"], sends=sends))
    for off in Y_ARRIVE:
        for d, last in (("L", 4), ("S", 3)):
            for k in range(1, last + 1):
                event = ("Bz", d, k, off)
                sends = [("z", ("Bz", d, k + 1, off))] if k < last else []
                ops.append(Op(event, waits=[event], after=["start"], sends=sends))
    return ops


LATE = (-3, 3, -4)


def scatter_ops():
    ops = []
    TO.clear()
    TO.update({("Az", n): v for n, v in SCATTER_TO.items()})
    TO.update({("By", n): SCATTER_TO[n] for n in (2, -1, 1)})
    for n, yo in enumerate(Y_LEAVE):
        sends = []
        if n == 0:
            sends = [("y", ("Ay", "L", 1, i)) for i in range(8)]
        ops.append(Op(("CA", n), sends=sends, cost=0.6, rank=2 + n))
    for i, zo in enumerate(Z_LEAVE):
        sends = []
        if i == 0:
            sends = [("z", ("Bz", "L", 1, j)) for j in range(4)]
        if i == 1:
            sends = [("z", ("Bz", "S", 1, j)) for j in range(4)]
        ops.append(Op(("CB", i), sends=sends, cost=0.35, rank=2 + i / 2))
    for i, off in enumerate(Z_LEAVE):
        ops.append(Op(("FA", i), waits=[("Ay", "L", 1, i)], after=[("CA", 0), ("CA", 1), ("CA", 2)], sends=[("y", ("Ay", "L", 2, i)), ("y", ("Ay", "S", 1, i))]))
        waits = [("Ay", "L", 2, i), ("Ay", "S", 1, i)]
        waits += [("Az", n) for n in {2: (4, 3), -2: (-3,), 0: (2, -2, 1, -1)}.get(off, ())]
        sends = [("z", ("Az", off))] if off else [("x", ("X", 0, k)) for k in range(3)]
        ops.append(Op(("TA", i), waits=waits, after=[("CA", 3)], sends=sends))
    for i in range(2, 8):
        for j, off in enumerate(Y_LEAVE):
            if i < 7:
                waits = [("Bz", "LS"[i % 2], i // 2, j)]
                sends = [("z", ("Bz", "LS"[i % 2], i // 2 + 1, j))]
            else:
                waits = [("Bz", "L", 4, j), ("Bz", "S", 3, j)]
                sends = [("y", ("By", off))]
                if off == 0:
                    waits += [("By", 2), ("By", -1), ("By", 1)]
                    sends = [("x", ("X", 1, k)) for k in range(3)]
            ops.append(Op(("FB", i, j), waits=waits, after=[("CB", i)], sends=sends))
    for ab in range(2):
        ops.append(Op(("X", ab), waits=[("X", ab, k) for k in range(3)], sends=[("s", ("G", ab))]))
    for ab in range(2):
        ops.append(Op(("W", ab), waits=[("G", ab)]))
    ops.append(Op("loss", after=[("CA", 3), ("CB", 7)], cost=1.0, rank=20, sends=[("s", ("l1",))]))
    ops.append(Op("pair", waits=[("l1",)], sends=[("x", ("l2", k)) for k in range(3)]))
    ops.append(Op("total", waits=[("l2", k) for k in range(3)]))
    for n in range(4):
        ops.append(Op(("attn", n), after=[("CA", 3), ("CB", 7)], cost=1.2, rank=30 + n))
    return ops


def size(event):
    if event[0] in ("l1", "l2"):
        return 0.05
    if event[0] == "X":
        return (0.73, 0.37)[event[1]]
    if event[0] == "G":
        return 0.15
    return (0.533 if event[0][0] == "A" else 0.267) * hops(event)


GATHER = order(gather_ops(), size)
SCATTER = order(scatter_ops(), size)
G_ID = {e: n for n, e in enumerate(e for op in GATHER for _, e in op.sends)}
S_ID = {e: n for n, e in enumerate(e for op in SCATTER for _, e in op.sends)}


def kernel(
    x_hbm, o_hbm, e_hbm, w_hbm, gain_hbm, len_hbm, pid_hbm, off_hbm, prow_hbm,
    rg_out, ag_out, wg_ref, loss_ref,
    wbuf, xb, ob, eb, ot, mixed, ss_ref, t_ref, g, gall,
    da, db, sa, ra, sa2, ra2, sb, rb, sb2, rb2,
    xra, xrb, xga, xgb, my, mz, msg1, msg2, ls, lx, lmsg1, lmsg2, crow,
    gain_in, gain_ref, len_ref, pid_ref, off_ref, prow_ref, gauge_a, gauge_b,
    loc, g_send, g_recv, b_send, b_recv, o_send, o_recv, h_send, h_recv, r_recv,
    a_send, a2_send, s_send, s2_send, x_send, q_send, y_send, y_recv, z_send, z_recv, l_send, m_send,
):
    gi, fi = lax.axis_index("group"), lax.axis_index("fsdp")
    x, c = gi // 2, lax.rem(gi, 2)
    z, y = fi // 4, lax.rem(fi, 4)
    s = 1 - 2 * c

    z_off = {off: lax.rem(z + off * s + 2 * NZ, NZ) for off in range(-4, 5)}
    y_off = {off: lax.rem(y + off * s + 2 * NY, NY) for off in range(-2, 3)}
    zat, yat = z_off.get, y_off.get

    def dev(xx, cc, zz, yy):
        return (xx * 2 + cc, zz * 4 + yy)

    def peer(event, to):
        kind, d = event[:2]
        if kind in ("Az", "By"):
            return dev(x, c, zat(to[d]), y) if kind == "Az" else dev(x, c, z, yat(to[d]))
        step = {"L": 1, "S": -1, "D": 2}[d]
        return dev(x, c, zat(step), y) if kind == "Bz" else dev(x, c, z, yat(step))

    sibling = dev(x, 1 - c, z, y)
    xs = [lax.rem(x + k, NX) for k in range(1, NX)]
    ys = [lax.rem(y + k, NY) for k in range(1, NY)]
    zs = [lax.rem(z + k, NZ) for k in range(1, NZ)]

    def remote(src, dst, send, recv, to):
        return pltpu.make_async_remote_copy(
            src_ref=src, dst_ref=dst, send_sem=send, recv_sem=recv, device_id=to, device_id_type=MESH
        )

    sent = []

    def start(copy):
        copy.start()
        sent.append(copy)

    loads = [
        pltpu.make_async_copy(w_hbm.at[:, 0:H], wbuf.at[0, z, y], loc.at[0]),
        pltpu.make_async_copy(w_hbm.at[:, H:D], wbuf.at[1, z, y], loc.at[1]),
        pltpu.make_async_copy(o_hbm, ob, loc.at[2]),
        pltpu.make_async_copy(x_hbm, xb, loc.at[3]),
        pltpu.make_async_copy(e_hbm, eb, loc.at[4]),
        pltpu.make_async_copy(gain_hbm, gain_in, loc.at[5]),
        pltpu.make_async_copy(len_hbm, len_ref, loc.at[6]),
        pltpu.make_async_copy(pid_hbm, pid_ref, loc.at[7]),
        pltpu.make_async_copy(off_hbm, off_ref, loc.at[8]),
        pltpu.make_async_copy(prow_hbm, prow_ref, loc.at[9]),
    ]
    for copy in loads:
        copy.start()

    barrier = pltpu.get_barrier_semaphore()
    greet = [sibling]
    greet += [dev(v, c, z, y) for v in xs] + [dev(x, c, z, v) for v in ys] + [dev(x, c, v, y) for v in zs]
    for to in greet:
        pl.semaphore_signal(barrier, inc=1, device_id=to, device_id_type=MESH)
    pl.semaphore_wait(barrier, len(greet))

    loads[0].wait()
    loads[1].wait()

    def block_of(event, sender):
        kind = event[0]
        if kind in ("Az", "By"):
            step = event[1]
            if sender:
                step += GATHER_TO[step]
            zz, yy = (zat(step), y) if kind == "Az" else (z, yat(step))
        else:
            d, k, off = event[1:]
            k = (0 if d == "D" else k - 1) if sender else k
            step = k if d == "S" else -k
            zz, yy = (zat(off), yat(step)) if kind == "Ay" else (zat(step), yat(off))
        cols = pl.ds(0, QA) if kind[0] == "A" else pl.ds(QA, QB)
        return wbuf.at[c, zz, yy, :, cols]

    def turn(n):
        piece = ob[:, pl.ds(n * Q, Q)].T
        ot[2 * n : 2 * n + 2, :, :, 0:TOK] = piece.reshape(2, 4, RB, TOK)
        part = ot.at[2 * n : 2 * n + 2, :, :, 0:TOK]
        start(remote(part, ot.at[2 * n : 2 * n + 2, :, :, TOK : 2 * TOK], o_send.at[n], o_recv.at[n], sibling))

    turn_at = {4: 0, 10: 1, 18: 2, 26: 3}
    for step, op in enumerate(GATHER):
        for event in op.waits:
            mine = block_of(event, False)
            remote(mine, mine, g_send.at[0], g_recv.at[G_ID[event]], sibling).wait_recv()
        for axis, event in op.sends:
            part = 0 if event[0][0] == "A" else 1
            blk = block_of(event, True)
            remote(blk, blk, g_send.at[part], g_recv.at[G_ID[event]], peer(event, GATHER_TO)).start()
        for event in op.waits:
            part = 0 if event[0][0] == "A" else 1
            mine = block_of(event, False)
            remote(mine, mine, b_send.at[part], b_recv.at[part], sibling).start()
        if step == 0:
            loads[2].wait()
        if step in turn_at:
            turn(turn_at[step])
    for part, gauge in enumerate((gauge_a, gauge_b)):
        remote(gauge, gauge, b_send.at[part], b_recv.at[part], sibling).wait_recv()
    for copy in loads[3:]:
        copy.wait()
    wide = gain_in[...].astype(F32)
    gain_ref[...] = jnp.concatenate([wide[n : n + 1] for n in range(D // 128)], axis=1)

    def forward(m, _):
        rows = pl.ds(pl.multiple_of(m * 160, 160), 160)
        ss = jnp.zeros((160, 1), F32)
        tt = jnp.zeros((160, 1), F32)
        for h in range(2):
            cols = pl.ds(h * H, H)
            w = wbuf[h].reshape(D, H)
            acc = jnp.dot(ob[rows, :], w, preferred_element_type=F32) + xb[rows, cols].astype(F32)
            mixed[h, rows, :] = acc
            eg = eb[rows, cols].astype(F32) * gain_ref[:, cols]
            ss = ss + jnp.sum(acc * acc, axis=1, keepdims=True)
            tt = tt + jnp.sum(acc * eg, axis=1, keepdims=True)
        ss_ref[rows, :] = jnp.broadcast_to(ss, (160, 128))
        t_ref[rows, :] = jnp.broadcast_to(tt, (160, 128))
        return 0

    lax.fori_loop(0, TOK // 160, forward, 0)

    first = (gi * 32 + fi) * 2
    lane = lax.broadcasted_iota(jnp.int32, (8, 128), 1)
    pos = lax.broadcasted_iota(jnp.int32, (SEQ, 128), 0)
    root = 1.0 / math.sqrt(D)
    deltas = []
    for j in range(2):
        rows = pl.ds(j * SEQ, SEQ)
        mask = (pos < len_ref[first + j]).astype(F32)
        scale = lax.rsqrt(ss_ref[rows, :] * (1.0 / D) + EPS)
        t = t_ref[rows, :]
        logp = t * scale * mask * root
        deltas.append(jnp.broadcast_to(jnp.sum(logp, axis=0, keepdims=True), (8, 128)) + off_ref[first + j])
        ss_ref[rows, :] = scale * mask * root
        t_ref[rows, :] = -(scale * scale * scale) * mask * (t * (root / D))
    at = lax.rem(gi, 2) * 64 + 2 * fi
    msg1[...] = jnp.where(lane == at, deltas[0], jnp.where(lane == at + 1, deltas[1], 0.0))

    def prepare(m, _):
        rows = pl.ds(pl.multiple_of(m * 64, 64), 64)
        ga = jnp.concatenate([ss_ref[rows, :]] * 6, axis=1)
        gb = jnp.concatenate([t_ref[rows, :]] * 6, axis=1)
        for h in range(2):
            cols = pl.ds(h * H, H)
            eg = eb[rows, cols].astype(F32) * gain_ref[:, cols]
            mixed[h, rows, :] = ga * eg + gb * mixed[h, rows, :]
        return 0

    for k in range(3):
        start(remote(msg1, my.at[k], y_send.at[k], y_recv.at[k], dev(x, c, z, ys[k])))
    lax.fori_loop(0, 4, prepare, 0)
    total = msg1[...]
    for k in range(3):
        remote(my.at[k], my.at[k], y_send.at[k], y_recv.at[k], sibling).wait_recv()
        total = total + my[k]
    msg2[...] = total
    for k in range(7):
        start(remote(msg2, mz.at[k], z_send.at[k], z_recv.at[k], dev(x, c, zs[k], y)))
    lax.fori_loop(4, 10, prepare, 0)
    for part, gauge in enumerate((gauge_a, gauge_b)):
        remote(gauge, gauge, g_send.at[part], g_recv.at[0], sibling).wait_send()
        remote(gauge, gauge, b_send.at[part], g_recv.at[0], sibling).wait_send()
    for k in range(7):
        remote(mz.at[k], mz.at[k], z_send.at[k], z_recv.at[k], sibling).wait_recv()
        total = total + mz[k]

    prow = jnp.broadcast_to(prow_ref[pl.ds(gi // 2, 1), :], (8, 128))
    for j in range(2):
        base = jnp.sum(jnp.where(prow == pid_ref[first + j], total, 0.0), axis=1, keepdims=True) * (1.0 / SAMPLES)
        crow[j] = deltas[j] - base

    def gradient(m, _):
        rows = pl.ds(pl.multiple_of(m * 64, 64), 64)
        cc = jnp.where(m < 5, crow[0], crow[1])[0:1]
        cc = jnp.concatenate([cc] * 6, axis=1)
        for h in range(2):
            value = (mixed[h, rows, :] * cc).astype(BF16)
            g[h, rows, :] = value
            rg_out[rows, h * H : (h + 1) * H] = value
        gall[rows, :] = g[c, rows, :]
        return 0

    lax.fori_loop(0, TOK // 64, gradient, 0)
    start(remote(g.at[1 - c], gall.at[pl.ds(TOK, TOK)], h_send.at[0], h_recv.at[0], sibling))
    for n in range(4):
        theirs = ot.at[2 * n : 2 * n + 2, :, :, TOK : 2 * TOK]
        remote(theirs, theirs, o_send.at[n], o_recv.at[n], sibling).wait_recv()
    theirs = gall.at[pl.ds(TOK, TOK)]
    remote(theirs, theirs, h_send.at[0], h_recv.at[0], sibling).wait_recv()

    def slot(event):
        kind, d = event[:2]
        if kind == "Ay":
            n = (0 if d == "L" else 2) + event[2] - 1
            return sa.at[n, event[3]], ra.at[n, event[3]], a_send
        if kind == "Az":
            n = list(SCATTER_TO).index(d)
            return sa2.at[n], ra2.at[n], a2_send
        if kind == "Bz":
            n = (0 if d == "L" else 4) + event[2] - 1
            return sb.at[n, event[3]], rb.at[n, event[3]], s_send
        n = (2, -1, 1).index(d)
        return sb2.at[n], rb2.at[n], s2_send

    def push(event, value):
        src, dst, sem = slot(event)
        src[...] = value.astype(BF16)
        remote(src, dst, sem.at[0], r_recv.at[S_ID[event]], peer(event, SCATTER_TO)).start()

    xr, xg = (xra, xrb), (xga, xgb)

    def got_of(event):
        if event[0] == "X":
            return xr[event[1]].at[lax.rem(x + NX - 1 - event[2], NX)]
        if event[0] == "G":
            return xg[event[1]].at[1 - c]
        if event[0] == "l1":
            return ls
        if event[0] == "l2":
            return lx.at[lax.rem(x + NX - 1 - event[1], NX)]
        return slot(event)[1]

    def spread(ab, value):
        xr[ab][x] = value.astype(BF16)
        for k in range(3):
            blk = xr[ab].at[x]
            remote(blk, blk, x_send.at[ab], r_recv.at[S_ID["X", ab, k]], dev(xs[k], c, z, y)).start()

    for op in SCATTER:
        got = 0.0
        for event in op.waits:
            dst = got_of(event)
            remote(dst, dst, a_send.at[0], r_recv.at[S_ID[event]], sibling).wait_recv()
            if event[0] in ("Ay", "Az", "By", "Bz"):
                got = got + dst[...].astype(F32)
        kind = op.key[0] if isinstance(op.key, tuple) else op.key
        if kind == "CA":
            yy = yat(Y_LEAVE[op.key[1]])
            lhs = ot[:, yy].reshape(8 * RB, 2 * TOK)
            da[:, yy] = jnp.dot(lhs, gall[:, 0:QA], preferred_element_type=F32).reshape(8, RB, QA)
            for axis, event in op.sends:
                push(event, da[zat(Z_LEAVE[event[3]]), yy])
        elif kind == "CB":
            zz = zat(Z_LEAVE[op.key[1]])
            lhs = ot[zz].reshape(4 * RB, 2 * TOK)
            db[zz] = jnp.dot(lhs, gall[:, QA:H], preferred_element_type=F32).reshape(4, RB, QB)
            for axis, event in op.sends:
                push(event, db[zz, yat(Y_LEAVE[event[3]])])
        elif kind == "FA":
            push(op.sends[0][1], da[zat(Z_LEAVE[op.key[1]]), yat(1)] + got)
            push(op.sends[1][1], da[zat(Z_LEAVE[op.key[1]]), yat(-1)])
        elif kind == "TA":
            value = da[zat(Z_LEAVE[op.key[1]]), y] + got
            if Z_LEAVE[op.key[1]]:
                push(op.sends[0][1], value)
            else:
                spread(0, value)
        elif kind == "FB":
            value = db[zat(Z_LEAVE[op.key[1]]), yat(Y_LEAVE[op.key[2]])] + got
            if op.sends[0][0] != "x":
                push(op.sends[0][1], value)
            else:
                spread(1, value)
        elif kind == "X":
            ab = op.key[1]
            part = [xr[ab][n].astype(F32) for n in range(NX)]
            value = ((part[0] + part[1]) + (part[2] + part[3])) * (1.0 / 512.0)
            xg[ab][c] = value
            blk = xg[ab].at[c]
            start(remote(blk, blk, q_send.at[ab], r_recv.at[S_ID["G", ab]], sibling))
        elif kind == "W":
            ab = op.key[1]
            for h in range(2):
                wg_ref[:, pl.ds(h * H + ab * QA, (QA, QB)[ab])] = xg[ab][h]
        elif kind == "pair":
            pair = lmsg1[...] + ls[...]
            lmsg2[...] = pair
            lx[x] = pair
            for k in range(3):
                start(remote(lmsg2, lx.at[x], m_send.at[k], r_recv.at[S_ID["l2", k]], dev(xs[k], c, z, y)))
        elif kind == "total":
            whole = (lx[0] + lx[1]) + (lx[2] + lx[3])
            loss_ref[0, 0] = jnp.sum(whole[0:1, 0:1]) * (1.0 / (512 * SEQ))
        elif kind == "attn":
            n = op.key[1]
            cols = pl.ds(n * Q, Q)
            w0 = wbuf[0, 2 * n : 2 * n + 2].reshape(Q, H)
            w1 = wbuf[1, 2 * n : 2 * n + 2].reshape(Q, H)
            dims = (((1,), (1,)), ((), ()))
            acc = lax.dot_general(g[0], w0, dims, preferred_element_type=F32)
            acc = acc + lax.dot_general(g[1], w1, dims, preferred_element_type=F32)
            ag_out[:, cols] = acc.astype(BF16)
        else:
            square = jnp.zeros((8, 1), F32)
            for p in range(PPG):
                member = prow == gi * PPG + p
                base = jnp.sum(jnp.where(member, total, 0.0), axis=1, keepdims=True) * (1.0 / SAMPLES)
                off = jnp.where(member, total - base, 0.0)
                square = square + jnp.sum(off * off, axis=1, keepdims=True)
            lmsg1[...] = jnp.broadcast_to(square, (8, 128))
            start(remote(lmsg1, ls, l_send.at[0], r_recv.at[S_ID[("l1",)]], sibling))

    for ref, sem in ((sa, a_send), (sa2, a2_send), (sb, s_send), (sb2, s2_send)):
        remote(ref, ref, sem.at[0], r_recv.at[0], sibling).wait_send()
    for ab in range(2):
        ref = xr[ab].at[0:3]
        remote(ref, ref, x_send.at[ab], r_recv.at[0], sibling).wait_send()
    for copy in sent:
        copy.wait_send()


def local(
    resid_in, attn_out, target_rows, out_weight, norm_gain,
    seq_lengths, prompt_ids, log_offsets, plan_dest, plan_slot,
):
    hbm = pl.BlockSpec(memory_space=pl.ANY)
    vmem = pl.BlockSpec(memory_space=pltpu.VMEM)
    smem = pl.BlockSpec(memory_space=pltpu.SMEM)
    dma = pltpu.SemaphoreType.DMA
    n_g, n_s = len(G_ID), len(S_ID)
    scratch = [
        pltpu.VMEM((2, NZ, NY, RB, H), BF16),
        pltpu.VMEM((TOK, D), BF16),
        pltpu.VMEM((TOK, D), BF16),
        pltpu.VMEM((TOK, D), BF16),
        pltpu.VMEM((NZ, NY, RB, 2 * TOK), BF16),
        pltpu.VMEM((2, TOK, H), F32),
        pltpu.VMEM((TOK, 128), F32),
        pltpu.VMEM((TOK, 128), F32),
        pltpu.VMEM((2, TOK, H), BF16),
        pltpu.VMEM((2 * TOK, H), BF16),
        pltpu.VMEM((NZ, NY, RB, QA), F32),
        pltpu.VMEM((NZ, NY, RB, QB), F32),
        pltpu.VMEM((3, 8, RB, QA), BF16),
        pltpu.VMEM((3, 8, RB, QA), BF16),
        pltpu.VMEM((7, RB, QA), BF16),
        pltpu.VMEM((7, RB, QA), BF16),
        pltpu.VMEM((7, 4, RB, QB), BF16),
        pltpu.VMEM((7, 4, RB, QB), BF16),
        pltpu.VMEM((3, RB, QB), BF16),
        pltpu.VMEM((3, RB, QB), BF16),
        pltpu.VMEM((4, RB, QA), BF16),
        pltpu.VMEM((4, RB, QB), BF16),
        pltpu.VMEM((2, RB, QA), F32),
        pltpu.VMEM((2, RB, QB), F32),
        pltpu.VMEM((3, 8, 128), F32),
        pltpu.VMEM((7, 8, 128), F32),
        pltpu.VMEM((8, 128), F32),
        pltpu.VMEM((8, 128), F32),
        pltpu.VMEM((8, 128), F32),
        pltpu.VMEM((4, 8, 128), F32),
        pltpu.VMEM((8, 128), F32),
        pltpu.VMEM((8, 128), F32),
        pltpu.VMEM((2, 8, 128), F32),
        pltpu.VMEM((D // 128, 128), BF16),
        pltpu.VMEM((1, D), F32),
        pltpu.SMEM((512,), jnp.int32),
        pltpu.SMEM((512,), jnp.int32),
        pltpu.SMEM((512,), F32),
        pltpu.VMEM((4, 128), jnp.int32),
        pltpu.VMEM((31, RB, QA), BF16),
        pltpu.VMEM((31, RB, QB), BF16),
        dma((10,)),
        dma((2,)), dma((n_g,)), dma((2,)), dma((2,)),
        dma((4,)), dma((4,)), dma((1,)), dma((1,)),
        dma((n_s,)),
        dma((1,)), dma((1,)), dma((1,)), dma((1,)), dma((2,)), dma((2,)),
        dma((3,)), dma((3,)), dma((7,)), dma((7,)),
        dma((1,)), dma((3,)),
    ]
    call = pl.pallas_call(
        kernel,
        out_shape=(
            pltpu.VMEM((TOK, D), BF16),
            pltpu.VMEM((TOK, D), BF16),
            pltpu.VMEM((RB, D), F32),
            jax.ShapeDtypeStruct((1, 1), F32),
        ),
        in_specs=[hbm] * 9,
        out_specs=(vmem, vmem, vmem, smem),
        scratch_shapes=scratch,
        name="balance",
        compiler_params=pltpu.CompilerParams(
            collective_id=0, has_side_effects=True, vmem_limit_bytes=48 * 1024 * 1024
        ),
        cost_estimate=pl.CostEstimate(flops=9060000000, bytes_accessed=10000000, transcendentals=640),
    )
    operands = (
        resid_in.reshape(TOK, D),
        attn_out.reshape(TOK, D),
        target_rows.reshape(TOK, D),
        out_weight,
        norm_gain.reshape(D // 128, 128),
        seq_lengths,
        prompt_ids,
        log_offsets,
        prompt_ids.reshape(4, 128),
    )
    rg, ag, wg, loss = call(*(pltpu.with_memory_space_constraint(v, pltpu.HBM) for v in operands))
    return rg.reshape(2, SEQ, D), ag.reshape(2, SEQ, D), wg, loss.reshape(())


def solution(mesh):
    return jax.shard_map(
        local,
        mesh=mesh,
        in_specs=(
            P(("group", "fsdp"), None, None),
            P(("group", "fsdp"), None, None),
            P(("group", "fsdp"), None, None),
            P("fsdp", None),
            P(), P(), P(), P(), P(), P(),
        ),
        out_specs=(
            P(("group", "fsdp"), None, None),
            P(("group", "fsdp"), None, None),
            P("fsdp", None),
            P(),
        ),
        check_vma=False,
    )
```

```python
import functools
import math

import jax
import jax.numpy as jnp
from jax import lax
from jax.experimental import pallas as pl
from jax.experimental.pallas import tpu as pltpu
from jax.sharding import PartitionSpec as P

MESH = pl.DeviceIdType.MESH
F32, BF16 = jnp.float32, jnp.bfloat16
NX, NC, NZ, NY = 4, 2, 8, 4
EPS = 1e-06
PPG = 8
SAMPLES = 8
D = 1536
TOK = 640
SEQ = 320
H = D // 2
Q = D // 4
QA, QB = 512, 256
RB = 48

Z_ARRIVE = (0, -1, 1, -2, 2, -3, 3, -4)
Y_ARRIVE = (0, -1, 1, -2)
Z_LEAVE = (4, -3, 3, -2, 2, -1, 1, 0)
Y_LEAVE = (2, -1, 1, 0)


class Op:
    def __init__(self, key, waits=(), after=(), sends=(), cost=0.2, rank=0):
        self.key, self.waits, self.after, self.sends, self.cost, self.rank = key, waits, after, sends, cost, rank


def order(ops, size):
    now, done, at, free, out = 0.0, set(), {}, {}, []
    left = list(ops)
    while left:
        best = None
        for n, op in enumerate(left):
            if all(a in done for a in op.after) and all(w in at for w in op.waits):
                ready = max([now] + [at[w] for w in op.waits])
                score = (ready, op.rank, n)
                if best is None or score < best[0]:
                    best = (score, op)
        (ready, _, _), op = best
        left.remove(op)
        now = ready + op.cost
        for axis, event in op.sends:
            free[axis] = max(now, free.get(axis, 0.0)) + size(event)
            at[event] = free[axis] + (0.9 if axis == "s" else 3.2 if size(event) > 0.6 else 2.8)
        done.add(op.key)
        out.append(op)
    return out


def hops(event):
    return abs(TO[event[0], event[1]]) if event[0] in ("Az", "By") else 2 if event[1] == "D" else 1


GATHER_TO = {-1: 1, 1: -1, -2: 2, 2: -2, -3: 1, 3: -1, -4: 2}
SCATTER_TO = {4: 2, 3: 1, -3: -1, -2: -2, 2: 2, -1: -1, 1: 1}
TO = {}


def gather_ops():
    ops = []
    TO.clear()
    TO.update({("Az", n): v for n, v in GATHER_TO.items()})
    TO.update({("By", n): GATHER_TO[n] for n in (-1, 1, -2)})

    def a_first(off):
        sends = [("y", ("Ay", "L", 1, off)), ("y", ("Ay", "S", 1, off))]
        if off in LATE:
            sends.append(("y", ("Ay", "D", 2, off)))
        if off == 0:
            sends = [("z", ("Az", n)) for n in (-2, 2, -1, 1)] + sends
        if off == -2:
            sends = [("z", ("Az", -4)), ("z", ("Az", -3))] + sends
        if off == 2:
            sends = [("z", ("Az", 3))] + sends
        return sends

    def b_first(off):
        sends = [("z", ("Bz", "L", 1, off)), ("z", ("Bz", "S", 1, off))]
        if off == 0:
            sends = [("y", ("By", n)) for n in (-2, -1, 1)] + sends
        return sends

    ops.append(Op("start", sends=a_first(0)[:4] + b_first(0) + a_first(0)[4:]))
    for off in Z_ARRIVE[1:]:
        ops.append(Op(("Az", off), waits=[("Az", off)], after=["start"], sends=a_first(off)))
    for off in Y_ARRIVE[1:]:
        ops.append(Op(("By", off), waits=[("By", off)], after=["start"], sends=b_first(off)))
    for off in Z_ARRIVE:
        for d, k in (("L", 1), ("D", 2) if off in LATE else ("L", 2), ("S", 1)):
            event = ("Ay", d, k, off)
            sends = [("y", ("Ay", d, k + 1, off))] if k == 1 and d == "L" and off not in LATE else []
            ops.append(Op(event, waits=[event], after=["start"], sends=sends))
    for off in Y_ARRIVE:
        for d, last in (("L", 4), ("S", 3)):
            for k in range(1, last + 1):
                event = ("Bz", d, k, off)
                sends = [("z", ("Bz", d, k + 1, off))] if k < last else []
                ops.append(Op(event, waits=[event], after=["start"], sends=sends))
    return ops


LATE = (-2, 2, -3, 3, -4)


def scatter_ops():
    ops = []
    TO.clear()
    TO.update({("Az", n): v for n, v in SCATTER_TO.items()})
    TO.update({("By", n): SCATTER_TO[n] for n in (2, -1, 1)})
    for n, yo in enumerate(Y_LEAVE):
        sends = []
        if n == 0:
            sends = [("y", ("Ay", "L", 1, i)) for i in range(8)]
        ops.append(Op(("CA", n), sends=sends, cost=0.6, rank=2 + n))
    for i, zo in enumerate(Z_LEAVE):
        sends = []
        if i == 0:
            sends = [("z", ("Bz", "L", 1, j)) for j in range(4)]
        if i == 1:
            sends = [("z", ("Bz", "S", 1, j)) for j in range(4)]
        ops.append(Op(("CB", i), sends=sends, cost=0.35, rank=2 + i / 2))
    for i, off in enumerate(Z_LEAVE):
        ops.append(Op(("FA", i), waits=[("Ay", "L", 1, i)], after=[("CA", 0), ("CA", 1), ("CA", 2)], sends=[("y", ("Ay", "L", 2, i)), ("y", ("Ay", "S", 1, i))]))
        waits = [("Ay", "L", 2, i), ("Ay", "S", 1, i)]
        waits += [("Az", n) for n in {2: (4, 3), -2: (-3,), 0: (2, -2, 1, -1)}.get(off, ())]
        sends = [("z", ("Az", off))] if off else [("x", ("X", 0, k)) for k in range(3)]
        ops.append(Op(("TA", i), waits=waits, after=[("CA", 3)], sends=sends))
    for i in range(2, 8):
        for j, off in enumerate(Y_LEAVE):
            if i < 7:
                waits = [("Bz", "LS"[i % 2], i // 2, j)]
                sends = [("z", ("Bz", "LS"[i % 2], i // 2 + 1, j))]
            else:
                waits = [("Bz", "L", 4, j), ("Bz", "S", 3, j)]
                sends = [("y", ("By", off))]
                if off == 0:
                    waits += [("By", 2), ("By", -1), ("By", 1)]
                    sends = [("x", ("X", 1, k)) for k in range(3)]
            ops.append(Op(("FB", i, j), waits=waits, after=[("CB", i)], sends=sends))
    for ab in range(2):
        ops.append(Op(("X", ab), waits=[("X", ab, k) for k in range(3)], sends=[("s", ("G", ab))]))
    for ab in range(2):
        ops.append(Op(("W", ab), waits=[("G", ab)]))
    ops.append(Op("loss", after=[("CA", 3), ("CB", 7)], cost=1.0, rank=20, sends=[("s", ("l1",))]))
    ops.append(Op("pair", waits=[("l1",)], sends=[("x", ("l2", k)) for k in range(3)]))
    ops.append(Op("total", waits=[("l2", k) for k in range(3)]))
    for n in range(4):
        ops.append(Op(("attn", n), after=[("CA", 3), ("CB", 7)], cost=1.2, rank=30 + n))
    return ops


def size(event):
    if event[0] in ("l1", "l2"):
        return 0.05
    if event[0] == "X":
        return (0.73, 0.37)[event[1]]
    if event[0] == "G":
        return 0.15
    return (0.533 if event[0][0] == "A" else 0.267) * hops(event)


GATHER = order(gather_ops(), size)
SCATTER = order(scatter_ops(), size)
G_ID = {e: n for n, e in enumerate(e for op in GATHER for _, e in op.sends)}
S_ID = {e: n for n, e in enumerate(e for op in SCATTER for _, e in op.sends)}


def kernel(
    x_hbm, o_hbm, e_hbm, w_hbm, gain_hbm, len_hbm, pid_hbm, off_hbm, prow_hbm,
    rg_out, ag_out, wg_ref, loss_ref,
    wbuf, xb, ob, eb, ot, mixed, ss_ref, t_ref, g, gall,
    da, db, sa, ra, sa2, ra2, sb, rb, sb2, rb2,
    xra, xrb, xga, xgb, my, mz, msg1, msg2, ls, lx, lmsg1, lmsg2, crow,
    gain_in, gain_ref, len_ref, pid_ref, off_ref, prow_ref, gauge_a, gauge_b,
    loc, g_send, g_recv, b_send, b_recv, o_send, o_recv, h_send, h_recv, r_recv,
    a_send, a2_send, s_send, s2_send, x_send, q_send, y_send, y_recv, z_send, z_recv, l_send, m_send,
):
    gi, fi = lax.axis_index("group"), lax.axis_index("fsdp")
    x, c = gi // 2, lax.rem(gi, 2)
    z, y = fi // 4, lax.rem(fi, 4)
    s = 1 - 2 * c

    z_off = {off: lax.rem(z + off * s + 2 * NZ, NZ) for off in range(-4, 5)}
    y_off = {off: lax.rem(y + off * s + 2 * NY, NY) for off in range(-2, 3)}
    zat, yat = z_off.get, y_off.get

    def dev(xx, cc, zz, yy):
        return (xx * 2 + cc, zz * 4 + yy)

    def peer(event, to):
        kind, d = event[:2]
        if kind in ("Az", "By"):
            return dev(x, c, zat(to[d]), y) if kind == "Az" else dev(x, c, z, yat(to[d]))
        step = {"L": 1, "S": -1, "D": 2}[d]
        return dev(x, c, zat(step), y) if kind == "Bz" else dev(x, c, z, yat(step))

    sibling = dev(x, 1 - c, z, y)
    xs = [lax.rem(x + k, NX) for k in range(1, NX)]
    ys = [lax.rem(y + k, NY) for k in range(1, NY)]
    zs = [lax.rem(z + k, NZ) for k in range(1, NZ)]

    def remote(src, dst, send, recv, to):
        return pltpu.make_async_remote_copy(
            src_ref=src, dst_ref=dst, send_sem=send, recv_sem=recv, device_id=to, device_id_type=MESH
        )

    sent = []

    def start(copy):
        copy.start()
        sent.append(copy)

    loads = [
        pltpu.make_async_copy(w_hbm.at[:, 0:H], wbuf.at[0, z, y], loc.at[0]),
        pltpu.make_async_copy(w_hbm.at[:, H:D], wbuf.at[1, z, y], loc.at[1]),
        pltpu.make_async_copy(o_hbm, ob, loc.at[2]),
        pltpu.make_async_copy(x_hbm, xb, loc.at[3]),
        pltpu.make_async_copy(e_hbm, eb, loc.at[4]),
        pltpu.make_async_copy(gain_hbm, gain_in, loc.at[5]),
        pltpu.make_async_copy(len_hbm, len_ref, loc.at[6]),
        pltpu.make_async_copy(pid_hbm, pid_ref, loc.at[7]),
        pltpu.make_async_copy(off_hbm, off_ref, loc.at[8]),
        pltpu.make_async_copy(prow_hbm, prow_ref, loc.at[9]),
    ]
    for copy in loads:
        copy.start()

    barrier = pltpu.get_barrier_semaphore()
    greet = [sibling]
    greet += [dev(v, c, z, y) for v in xs] + [dev(x, c, z, v) for v in ys] + [dev(x, c, v, y) for v in zs]
    for to in greet:
        pl.semaphore_signal(barrier, inc=1, device_id=to, device_id_type=MESH)
    pl.semaphore_wait(barrier, len(greet))

    loads[0].wait()
    loads[1].wait()

    def block_of(event, sender):
        kind = event[0]
        if kind in ("Az", "By"):
            step = event[1]
            if sender:
                step += GATHER_TO[step]
            zz, yy = (zat(step), y) if kind == "Az" else (z, yat(step))
        else:
            d, k, off = event[1:]
            k = (0 if d == "D" else k - 1) if sender else k
            step = k if d == "S" else -k
            zz, yy = (zat(off), yat(step)) if kind == "Ay" else (zat(step), yat(off))
        cols = pl.ds(0, QA) if kind[0] == "A" else pl.ds(QA, QB)
        return wbuf.at[c, zz, yy, :, cols]

    def turn(n):
        piece = ob[:, pl.ds(n * Q, Q)].T
        ot[2 * n : 2 * n + 2, :, :, 0:TOK] = piece.reshape(2, 4, RB, TOK)
        part = ot.at[2 * n : 2 * n + 2, :, :, 0:TOK]
        start(remote(part, ot.at[2 * n : 2 * n + 2, :, :, TOK : 2 * TOK], o_send.at[n], o_recv.at[n], sibling))

    turn_at = {4: 0, 10: 1, 18: 2, 26: 3}
    for step, op in enumerate(GATHER):
        for event in op.waits:
            mine = block_of(event, False)
            remote(mine, mine, g_send.at[0], g_recv.at[G_ID[event]], sibling).wait_recv()
        for axis, event in op.sends:
            part = 0 if event[0][0] == "A" else 1
            blk = block_of(event, True)
            remote(blk, blk, g_send.at[part], g_recv.at[G_ID[event]], peer(event, GATHER_TO)).start()
        for event in op.waits:
            part = 0 if event[0][0] == "A" else 1
            mine = block_of(event, False)
            remote(mine, mine, b_send.at[part], b_recv.at[part], sibling).start()
        if step == 0:
            loads[2].wait()
        if step in turn_at:
            turn(turn_at[step])
    for part, gauge in enumerate((gauge_a, gauge_b)):
        remote(gauge, gauge, b_send.at[part], b_recv.at[part], sibling).wait_recv()
    for copy in loads[3:]:
        copy.wait()
    wide = gain_in[...].astype(F32)
    gain_ref[...] = jnp.concatenate([wide[n : n + 1] for n in range(D // 128)], axis=1)

    def forward(m, _):
        rows = pl.ds(pl.multiple_of(m * 320, 320), 320)
        ss = jnp.zeros((320, 1), F32)
        tt = jnp.zeros((320, 1), F32)
        for h in range(2):
            cols = pl.ds(h * H, H)
            w = wbuf[h].reshape(D, H)
            acc = jnp.dot(ob[rows, :], w, preferred_element_type=F32) + xb[rows, cols].astype(F32)
            mixed[h, rows, :] = acc
            eg = eb[rows, cols].astype(F32) * gain_ref[:, cols]
            ss = ss + jnp.sum(acc * acc, axis=1, keepdims=True)
            tt = tt + jnp.sum(acc * eg, axis=1, keepdims=True)
        ss_ref[rows, :] = jnp.broadcast_to(ss, (320, 128))
        t_ref[rows, :] = jnp.broadcast_to(tt, (320, 128))
        return 0

    lax.fori_loop(0, TOK // 320, forward, 0)

    first = (gi * 32 + fi) * 2
    lane = lax.broadcasted_iota(jnp.int32, (8, 128), 1)
    pos = lax.broadcasted_iota(jnp.int32, (SEQ, 128), 0)
    root = 1.0 / math.sqrt(D)
    deltas = []
    for j in range(2):
        rows = pl.ds(j * SEQ, SEQ)
        mask = (pos < len_ref[first + j]).astype(F32)
        scale = lax.rsqrt(ss_ref[rows, :] * (1.0 / D) + EPS)
        t = t_ref[rows, :]
        logp = t * scale * mask * root
        deltas.append(jnp.broadcast_to(jnp.sum(logp, axis=0, keepdims=True), (8, 128)) + off_ref[first + j])
        ss_ref[rows, :] = scale * mask * root
        t_ref[rows, :] = -(scale * scale * scale) * mask * (t * (root / D))
    at = lax.rem(gi, 2) * 64 + 2 * fi
    msg1[...] = jnp.where(lane == at, deltas[0], jnp.where(lane == at + 1, deltas[1], 0.0))

    def prepare(m, _):
        rows = pl.ds(pl.multiple_of(m * 64, 64), 64)
        ga = jnp.concatenate([ss_ref[rows, :]] * 6, axis=1)
        gb = jnp.concatenate([t_ref[rows, :]] * 6, axis=1)
        for h in range(2):
            cols = pl.ds(h * H, H)
            eg = eb[rows, cols].astype(F32) * gain_ref[:, cols]
            mixed[h, rows, :] = ga * eg + gb * mixed[h, rows, :]
        return 0

    for k in range(3):
        start(remote(msg1, my.at[k], y_send.at[k], y_recv.at[k], dev(x, c, z, ys[k])))
    lax.fori_loop(0, 4, prepare, 0)
    total = msg1[...]
    for k in range(3):
        remote(my.at[k], my.at[k], y_send.at[k], y_recv.at[k], sibling).wait_recv()
        total = total + my[k]
    msg2[...] = total
    for k in range(7):
        start(remote(msg2, mz.at[k], z_send.at[k], z_recv.at[k], dev(x, c, zs[k], y)))
    lax.fori_loop(4, 10, prepare, 0)
    for part, gauge in enumerate((gauge_a, gauge_b)):
        remote(gauge, gauge, g_send.at[part], g_recv.at[0], sibling).wait_send()
        remote(gauge, gauge, b_send.at[part], g_recv.at[0], sibling).wait_send()
    for k in range(7):
        remote(mz.at[k], mz.at[k], z_send.at[k], z_recv.at[k], sibling).wait_recv()
        total = total + mz[k]

    prow = jnp.broadcast_to(prow_ref[pl.ds(gi // 2, 1), :], (8, 128))
    for j in range(2):
        base = jnp.sum(jnp.where(prow == pid_ref[first + j], total, 0.0), axis=1, keepdims=True) * (1.0 / SAMPLES)
        crow[j] = deltas[j] - base

    def gradient(m, _):
        rows = pl.ds(pl.multiple_of(m * 64, 64), 64)
        cc = jnp.where(m < 5, crow[0], crow[1])[0:1]
        cc = jnp.concatenate([cc] * 6, axis=1)
        for h in range(2):
            value = (mixed[h, rows, :] * cc).astype(BF16)
            g[h, rows, :] = value
            rg_out[rows, h * H : (h + 1) * H] = value
        gall[rows, :] = g[c, rows, :]
        return 0

    lax.fori_loop(0, TOK // 64, gradient, 0)
    pieces = (pl.ds(0, QA), pl.ds(QA, QB))
    for n, cols in enumerate(pieces):
        theirs = gall.at[pl.ds(TOK, TOK), cols]
        start(remote(g.at[1 - c, :, cols], theirs, h_send.at[n], h_recv.at[n], sibling))
    for n in range(4):
        theirs = ot.at[2 * n : 2 * n + 2, :, :, TOK : 2 * TOK]
        remote(theirs, theirs, o_send.at[n], o_recv.at[n], sibling).wait_recv()
    taken = set()

    def take(n):
        if n not in taken:
            taken.add(n)
            theirs = gall.at[pl.ds(TOK, TOK), pieces[n]]
            remote(theirs, theirs, h_send.at[n], h_recv.at[n], sibling).wait_recv()

    def slot(event):
        kind, d = event[:2]
        if kind == "Ay":
            n = (0 if d == "L" else 2) + event[2] - 1
            return sa.at[n, event[3]], ra.at[n, event[3]], a_send
        if kind == "Az":
            n = list(SCATTER_TO).index(d)
            return sa2.at[n], ra2.at[n], a2_send
        if kind == "Bz":
            n = (0 if d == "L" else 4) + event[2] - 1
            return sb.at[n, event[3]], rb.at[n, event[3]], s_send
        n = (2, -1, 1).index(d)
        return sb2.at[n], rb2.at[n], s2_send

    def push(event, value):
        src, dst, sem = slot(event)
        src[...] = value.astype(BF16)
        remote(src, dst, sem.at[0], r_recv.at[S_ID[event]], peer(event, SCATTER_TO)).start()

    xr, xg = (xra, xrb), (xga, xgb)

    def got_of(event):
        if event[0] == "X":
            return xr[event[1]].at[lax.rem(x + NX - 1 - event[2], NX)]
        if event[0] == "G":
            return xg[event[1]].at[1 - c]
        if event[0] == "l1":
            return ls
        if event[0] == "l2":
            return lx.at[lax.rem(x + NX - 1 - event[1], NX)]
        return slot(event)[1]

    def spread(ab, value):
        xr[ab][x] = value.astype(BF16)
        for k in range(3):
            blk = xr[ab].at[x]
            remote(blk, blk, x_send.at[ab], r_recv.at[S_ID["X", ab, k]], dev(xs[k], c, z, y)).start()

    for op in SCATTER:
        got = 0.0
        for event in op.waits:
            dst = got_of(event)
            remote(dst, dst, a_send.at[0], r_recv.at[S_ID[event]], sibling).wait_recv()
            if event[0] in ("Ay", "Az", "By", "Bz"):
                got = got + dst[...].astype(F32)
        kind = op.key[0] if isinstance(op.key, tuple) else op.key
        if kind == "CA":
            take(0)
            yy = yat(Y_LEAVE[op.key[1]])
            lhs = ot[:, yy].reshape(8 * RB, 2 * TOK)
            da[:, yy] = jnp.dot(lhs, gall[:, 0:QA], preferred_element_type=F32).reshape(8, RB, QA)
            for axis, event in op.sends:
                push(event, da[zat(Z_LEAVE[event[3]]), yy])
        elif kind == "CB":
            take(1)
            zz = zat(Z_LEAVE[op.key[1]])
            lhs = ot[zz].reshape(4 * RB, 2 * TOK)
            db[zz] = jnp.dot(lhs, gall[:, QA:H], preferred_element_type=F32).reshape(4, RB, QB)
            for axis, event in op.sends:
                push(event, db[zz, yat(Y_LEAVE[event[3]])])
        elif kind == "FA":
            push(op.sends[0][1], da[zat(Z_LEAVE[op.key[1]]), yat(1)] + got)
            push(op.sends[1][1], da[zat(Z_LEAVE[op.key[1]]), yat(-1)])
        elif kind == "TA":
            value = da[zat(Z_LEAVE[op.key[1]]), y] + got
            if Z_LEAVE[op.key[1]]:
                push(op.sends[0][1], value)
            else:
                spread(0, value)
        elif kind == "FB":
            value = db[zat(Z_LEAVE[op.key[1]]), yat(Y_LEAVE[op.key[2]])] + got
            if op.sends[0][0] != "x":
                push(op.sends[0][1], value)
            else:
                spread(1, value)
        elif kind == "X":
            ab = op.key[1]
            part = [xr[ab][n].astype(F32) for n in range(NX)]
            value = ((part[0] + part[1]) + (part[2] + part[3])) * (1.0 / 512.0)
            xg[ab][c] = value
            blk = xg[ab].at[c]
            start(remote(blk, blk, q_send.at[ab], r_recv.at[S_ID["G", ab]], sibling))
        elif kind == "W":
            ab = op.key[1]
            for h in range(2):
                wg_ref[:, pl.ds(h * H + ab * QA, (QA, QB)[ab])] = xg[ab][h]
        elif kind == "pair":
            pair = lmsg1[...] + ls[...]
            lmsg2[...] = pair
            lx[x] = pair
            for k in range(3):
                start(remote(lmsg2, lx.at[x], m_send.at[k], r_recv.at[S_ID["l2", k]], dev(xs[k], c, z, y)))
        elif kind == "total":
            whole = (lx[0] + lx[1]) + (lx[2] + lx[3])
            loss_ref[0, 0] = jnp.sum(whole[0:1, 0:1]) * (1.0 / (512 * SEQ))
        elif kind == "attn":
            n = op.key[1]
            cols = pl.ds(n * Q, Q)
            w0 = wbuf[0, 2 * n : 2 * n + 2].reshape(Q, H)
            w1 = wbuf[1, 2 * n : 2 * n + 2].reshape(Q, H)
            dims = (((1,), (1,)), ((), ()))
            acc = lax.dot_general(g[0], w0, dims, preferred_element_type=F32)
            acc = acc + lax.dot_general(g[1], w1, dims, preferred_element_type=F32)
            ag_out[:, cols] = acc.astype(BF16)
        else:
            square = jnp.zeros((8, 1), F32)
            for p in range(PPG):
                member = prow == gi * PPG + p
                base = jnp.sum(jnp.where(member, total, 0.0), axis=1, keepdims=True) * (1.0 / SAMPLES)
                off = jnp.where(member, total - base, 0.0)
                square = square + jnp.sum(off * off, axis=1, keepdims=True)
            lmsg1[...] = jnp.broadcast_to(square, (8, 128))
            start(remote(lmsg1, ls, l_send.at[0], r_recv.at[S_ID[("l1",)]], sibling))

    for ref, sem in ((sa, a_send), (sa2, a2_send), (sb, s_send), (sb2, s2_send)):
        remote(ref, ref, sem.at[0], r_recv.at[0], sibling).wait_send()
    for ab in range(2):
        ref = xr[ab].at[0:3]
        remote(ref, ref, x_send.at[ab], r_recv.at[0], sibling).wait_send()
    for copy in sent:
        copy.wait_send()


def local(
    resid_in, attn_out, target_rows, out_weight, norm_gain,
    seq_lengths, prompt_ids, log_offsets, plan_dest, plan_slot,
):
    hbm = pl.BlockSpec(memory_space=pl.ANY)
    vmem = pl.BlockSpec(memory_space=pltpu.VMEM)
    smem = pl.BlockSpec(memory_space=pltpu.SMEM)
    dma = pltpu.SemaphoreType.DMA
    n_g, n_s = len(G_ID), len(S_ID)
    scratch = [
        pltpu.VMEM((2, NZ, NY, RB, H), BF16),
        pltpu.VMEM((TOK, D), BF16),
        pltpu.VMEM((TOK, D), BF16),
        pltpu.VMEM((TOK, D), BF16),
        pltpu.VMEM((NZ, NY, RB, 2 * TOK), BF16),
        pltpu.VMEM((2, TOK, H), F32),
        pltpu.VMEM((TOK, 128), F32),
        pltpu.VMEM((TOK, 128), F32),
        pltpu.VMEM((2, TOK, H), BF16),
        pltpu.VMEM((2 * TOK, H), BF16),
        pltpu.VMEM((NZ, NY, RB, QA), F32),
        pltpu.VMEM((NZ, NY, RB, QB), F32),
        pltpu.VMEM((3, 8, RB, QA), BF16),
        pltpu.VMEM((3, 8, RB, QA), BF16),
        pltpu.VMEM((7, RB, QA), BF16),
        pltpu.VMEM((7, RB, QA), BF16),
        pltpu.VMEM((7, 4, RB, QB), BF16),
        pltpu.VMEM((7, 4, RB, QB), BF16),
        pltpu.VMEM((3, RB, QB), BF16),
        pltpu.VMEM((3, RB, QB), BF16),
        pltpu.VMEM((4, RB, QA), BF16),
        pltpu.VMEM((4, RB, QB), BF16),
        pltpu.VMEM((2, RB, QA), F32),
        pltpu.VMEM((2, RB, QB), F32),
        pltpu.VMEM((3, 8, 128), F32),
        pltpu.VMEM((7, 8, 128), F32),
        pltpu.VMEM((8, 128), F32),
        pltpu.VMEM((8, 128), F32),
        pltpu.VMEM((8, 128), F32),
        pltpu.VMEM((4, 8, 128), F32),
        pltpu.VMEM((8, 128), F32),
        pltpu.VMEM((8, 128), F32),
        pltpu.VMEM((2, 8, 128), F32),
        pltpu.VMEM((D // 128, 128), BF16),
        pltpu.VMEM((1, D), F32),
        pltpu.SMEM((512,), jnp.int32),
        pltpu.SMEM((512,), jnp.int32),
        pltpu.SMEM((512,), F32),
        pltpu.VMEM((4, 128), jnp.int32),
        pltpu.VMEM((31, RB, QA), BF16),
        pltpu.VMEM((31, RB, QB), BF16),
        dma((10,)),
        dma((2,)), dma((n_g,)), dma((2,)), dma((2,)),
        dma((4,)), dma((4,)), dma((2,)), dma((2,)),
        dma((n_s,)),
        dma((1,)), dma((1,)), dma((1,)), dma((1,)), dma((2,)), dma((2,)),
        dma((3,)), dma((3,)), dma((7,)), dma((7,)),
        dma((1,)), dma((3,)),
    ]
    call = pl.pallas_call(
        kernel,
        out_shape=(
            pltpu.VMEM((TOK, D), BF16),
            pltpu.VMEM((TOK, D), BF16),
            pltpu.VMEM((RB, D), F32),
            jax.ShapeDtypeStruct((1, 1), F32),
        ),
        in_specs=[hbm] * 9,
        out_specs=(vmem, vmem, vmem, smem),
        scratch_shapes=scratch,
        name="balance",
        compiler_params=pltpu.CompilerParams(
            collective_id=0, has_side_effects=True, vmem_limit_bytes=48 * 1024 * 1024
        ),
        cost_estimate=pl.CostEstimate(flops=9060000000, bytes_accessed=10000000, transcendentals=640),
    )
    operands = (
        resid_in.reshape(TOK, D),
        attn_out.reshape(TOK, D),
        target_rows.reshape(TOK, D),
        out_weight,
        norm_gain.reshape(D // 128, 128),
        seq_lengths,
        prompt_ids,
        log_offsets,
        prompt_ids.reshape(4, 128),
    )
    rg, ag, wg, loss = call(*(pltpu.with_memory_space_constraint(v, pltpu.HBM) for v in operands))
    return rg.reshape(2, SEQ, D), ag.reshape(2, SEQ, D), wg, loss.reshape(())


def solution(mesh):
    return jax.shard_map(
        local,
        mesh=mesh,
        in_specs=(
            P(("group", "fsdp"), None, None),
            P(("group", "fsdp"), None, None),
            P(("group", "fsdp"), None, None),
            P("fsdp", None),
            P(), P(), P(), P(), P(), P(),
        ),
        out_specs=(
            P(("group", "fsdp"), None, None),
            P(("group", "fsdp"), None, None),
            P("fsdp", None),
            P(),
        ),
        check_vma=False,
    )
```

```python
import functools
import math

import jax
import jax.numpy as jnp
from jax import lax
from jax.experimental import pallas as pl
from jax.experimental.pallas import tpu as pltpu
from jax.sharding import PartitionSpec as P

MESH = pl.DeviceIdType.MESH
F32, BF16 = jnp.float32, jnp.bfloat16
NX, NC, NZ, NY = 4, 2, 8, 4
EPS = 1e-06
PPG = 8
SAMPLES = 8
D = 1536
TOK = 640
SEQ = 320
H = D // 2
Q = D // 4
QA, QB = 512, 256
RB = 48

Z_ARRIVE = (0, -1, 1, -2, 2, -3, 3, -4)
Y_ARRIVE = (0, -1, 1, -2)
Z_LEAVE = (4, -3, 3, -2, 2, -1, 1, 0)
Y_LEAVE = (2, -1, 1, 0)


class Op:
    def __init__(self, key, waits=(), after=(), sends=(), cost=0.2, rank=0):
        self.key, self.waits, self.after, self.sends, self.cost, self.rank = key, waits, after, sends, cost, rank


def order(ops, size):
    now, done, at, free, out = 0.0, set(), {}, {}, []
    left = list(ops)
    while left:
        best = None
        for n, op in enumerate(left):
            if all(a in done for a in op.after) and all(w in at for w in op.waits):
                ready = max([now] + [at[w] for w in op.waits])
                score = (ready, op.rank, n)
                if best is None or score < best[0]:
                    best = (score, op)
        (ready, _, _), op = best
        left.remove(op)
        now = ready + op.cost
        for axis, event in op.sends:
            free[axis] = max(now, free.get(axis, 0.0)) + size(event)
            at[event] = free[axis] + (0.9 if axis == "s" else 3.2 if size(event) > 0.6 else 2.8)
        done.add(op.key)
        out.append(op)
    return out


def hops(event):
    return abs(TO[event[0], event[1]]) if event[0] in ("Az", "By") else 2 if event[1] == "D" else 1


GATHER_TO = {-1: 1, 1: -1, -2: 2, 2: -2, -3: 1, 3: -1, -4: 2}
SCATTER_TO = {4: 2, 3: 1, -3: -1, -2: -2, 2: 2, -1: -1, 1: 1}
TO = {}


def gather_ops():
    ops = []
    TO.clear()
    TO.update({("Az", n): v for n, v in GATHER_TO.items()})
    TO.update({("By", n): GATHER_TO[n] for n in (-1, 1, -2)})

    def a_first(off):
        sends = [("y", ("Ay", "L", 1, off)), ("y", ("Ay", "S", 1, off))]
        if off in LATE:
            sends.append(("y", ("Ay", "D", 2, off)))
        if off == 0:
            sends = [("z", ("Az", n)) for n in (-2, 2, -1, 1)] + sends
        if off == -2:
            sends = [("z", ("Az", -4)), ("z", ("Az", -3))] + sends
        if off == 2:
            sends = [("z", ("Az", 3))] + sends
        return sends

    def b_first(off):
        sends = [("z", ("Bz", "L", 1, off)), ("z", ("Bz", "S", 1, off))]
        if off == 0:
            sends = [("y", ("By", n)) for n in (-2, -1, 1)] + sends
        return sends

    ops.append(Op("start", sends=a_first(0)[:4] + b_first(0) + a_first(0)[4:]))
    for off in Z_ARRIVE[1:]:
        ops.append(Op(("Az", off), waits=[("Az", off)], after=["start"], sends=a_first(off)))
    for off in Y_ARRIVE[1:]:
        ops.append(Op(("By", off), waits=[("By", off)], after=["start"], sends=b_first(off)))
    for off in Z_ARRIVE:
        for d, k in (("L", 1), ("D", 2) if off in LATE else ("L", 2), ("S", 1)):
            event = ("Ay", d, k, off)
            sends = [("y", ("Ay", d, k + 1, off))] if k == 1 and d == "L" and off not in LATE else []
            ops.append(Op(event, waits=[event], after=["start"], sends=sends))
    for off in Y_ARRIVE:
        for d, last in (("L", 4), ("S", 3)):
            for k in range(1, last + 1):
                event = ("Bz", d, k, off)
                sends = [("z", ("Bz", d, k + 1, off))] if k < last else []
                ops.append(Op(event, waits=[event], after=["start"], sends=sends))
    return ops


LATE = (-2, 2, -3, 3, -4)


def scatter_ops():
    ops = []
    TO.clear()
    TO.update({("Az", n): v for n, v in SCATTER_TO.items()})
    TO.update({("By", n): SCATTER_TO[n] for n in (2, -1, 1)})
    for n, yo in enumerate(Y_LEAVE):
        sends = []
        if n == 0:
            sends = [("y", ("Ay", "L", 1, i)) for i in range(8)]
        ops.append(Op(("CA", n), sends=sends, cost=0.6, rank=2 + n))
    for i, zo in enumerate(Z_LEAVE):
        sends = []
        if i == 0:
            sends = [("z", ("Bz", "L", 1, j)) for j in range(4)]
        if i == 1:
            sends = [("z", ("Bz", "S", 1, j)) for j in range(4)]
        ops.append(Op(("CB", i), sends=sends, cost=0.35, rank=2 + i / 2))
    for i, off in enumerate(Z_LEAVE):
        ops.append(Op(("FA", i), waits=[("Ay", "L", 1, i)], after=[("CA", 0), ("CA", 1), ("CA", 2)], sends=[("y", ("Ay", "L", 2, i)), ("y", ("Ay", "S", 1, i))]))
        waits = [("Ay", "L", 2, i), ("Ay", "S", 1, i)]
        waits += [("Az", n) for n in {2: (4, 3), -2: (-3,), 0: (2, -2, 1, -1)}.get(off, ())]
        sends = [("z", ("Az", off))] if off else [("x", ("X", 0, k)) for k in range(3)]
        ops.append(Op(("TA", i), waits=waits, after=[("CA", 3)], sends=sends))
    for i in range(2, 8):
        for j, off in enumerate(Y_LEAVE):
            if i < 7:
                waits = [("Bz", "LS"[i % 2], i // 2, j)]
                sends = [("z", ("Bz", "LS"[i % 2], i // 2 + 1, j))]
            else:
                waits = [("Bz", "L", 4, j), ("Bz", "S", 3, j)]
                sends = [("y", ("By", off))]
                if off == 0:
                    waits += [("By", 2), ("By", -1), ("By", 1)]
                    sends = [("x", ("X", 1, k)) for k in range(3)]
            ops.append(Op(("FB", i, j), waits=waits, after=[("CB", i)], sends=sends))
    for ab in range(2):
        ops.append(Op(("X", ab), waits=[("X", ab, k) for k in range(3)], sends=[("s", ("G", ab))]))
    for ab in range(2):
        ops.append(Op(("W", ab), waits=[("G", ab)]))
    ops.append(Op("loss", after=[("CA", 3), ("CB", 7)], cost=1.0, rank=20, sends=[("s", ("l1",))]))
    ops.append(Op("pair", waits=[("l1",)], sends=[("x", ("l2", k)) for k in range(3)]))
    ops.append(Op("total", waits=[("l2", k) for k in range(3)]))
    for n in range(4):
        ops.append(Op(("attn", n), after=[("TA", 7), ("FB", 7, 3)], cost=1.2, rank=30 + n))
    return ops


def size(event):
    if event[0] in ("l1", "l2"):
        return 0.05
    if event[0] == "X":
        return (0.73, 0.37)[event[1]]
    if event[0] == "G":
        return 0.15
    return (0.533 if event[0][0] == "A" else 0.267) * hops(event)


GATHER = order(gather_ops(), size)
SCATTER = order(scatter_ops(), size)
G_ID = {e: n for n, e in enumerate(e for op in GATHER for _, e in op.sends)}
S_ID = {e: n for n, e in enumerate(e for op in SCATTER for _, e in op.sends)}


def kernel(
    x_hbm, o_hbm, e_hbm, w_hbm, gain_hbm, len_hbm, pid_hbm, off_hbm, prow_hbm,
    rg_out, ag_out, wg_ref, loss_ref,
    wbuf, xb, ob, eb, ot, mixed, ss_ref, t_ref, g, gall,
    da, db, sa, ra, sa2, ra2, sb, rb, sb2, rb2,
    xra, xrb, xga, xgb, my, mz, msg1, msg2, ls, lx, lmsg1, lmsg2, crow,
    gain_in, gain_ref, len_ref, pid_ref, off_ref, prow_ref, gauge_a, gauge_b,
    loc, g_send, g_recv, b_send, b_recv, o_send, o_recv, h_send, h_recv, r_recv,
    a_send, a2_send, s_send, s2_send, x_send, q_send, y_send, y_recv, z_send, z_recv, l_send, m_send,
):
    gi, fi = lax.axis_index("group"), lax.axis_index("fsdp")
    x, c = gi // 2, lax.rem(gi, 2)
    z, y = fi // 4, lax.rem(fi, 4)
    s = 1 - 2 * c

    z_off = {off: lax.rem(z + off * s + 2 * NZ, NZ) for off in range(-4, 5)}
    y_off = {off: lax.rem(y + off * s + 2 * NY, NY) for off in range(-2, 3)}
    zat, yat = z_off.get, y_off.get

    def dev(xx, cc, zz, yy):
        return (xx * 2 + cc, zz * 4 + yy)

    def peer(event, to):
        kind, d = event[:2]
        if kind in ("Az", "By"):
            return dev(x, c, zat(to[d]), y) if kind == "Az" else dev(x, c, z, yat(to[d]))
        step = {"L": 1, "S": -1, "D": 2}[d]
        return dev(x, c, zat(step), y) if kind == "Bz" else dev(x, c, z, yat(step))

    sibling = dev(x, 1 - c, z, y)
    xs = [lax.rem(x + k, NX) for k in range(1, NX)]
    ys = [lax.rem(y + k, NY) for k in range(1, NY)]
    zs = [lax.rem(z + k, NZ) for k in range(1, NZ)]

    def remote(src, dst, send, recv, to):
        return pltpu.make_async_remote_copy(
            src_ref=src, dst_ref=dst, send_sem=send, recv_sem=recv, device_id=to, device_id_type=MESH
        )

    sent = []

    def start(copy):
        copy.start()
        sent.append(copy)

    loads = [
        pltpu.make_async_copy(w_hbm.at[:, 0:H], wbuf.at[0, z, y], loc.at[0]),
        pltpu.make_async_copy(w_hbm.at[:, H:D], wbuf.at[1, z, y], loc.at[1]),
        pltpu.make_async_copy(o_hbm, ob, loc.at[2]),
        pltpu.make_async_copy(x_hbm, xb, loc.at[3]),
        pltpu.make_async_copy(e_hbm, eb, loc.at[4]),
        pltpu.make_async_copy(gain_hbm, gain_in, loc.at[5]),
        pltpu.make_async_copy(len_hbm, len_ref, loc.at[6]),
        pltpu.make_async_copy(pid_hbm, pid_ref, loc.at[7]),
        pltpu.make_async_copy(off_hbm, off_ref, loc.at[8]),
        pltpu.make_async_copy(prow_hbm, prow_ref, loc.at[9]),
    ]
    for copy in loads:
        copy.start()

    barrier = pltpu.get_barrier_semaphore()
    greet = [sibling]
    greet += [dev(v, c, z, y) for v in xs] + [dev(x, c, z, v) for v in ys] + [dev(x, c, v, y) for v in zs]
    for to in greet:
        pl.semaphore_signal(barrier, inc=1, device_id=to, device_id_type=MESH)
    pl.semaphore_wait(barrier, len(greet))

    loads[0].wait()
    loads[1].wait()

    def block_of(event, sender):
        kind = event[0]
        if kind in ("Az", "By"):
            step = event[1]
            if sender:
                step += GATHER_TO[step]
            zz, yy = (zat(step), y) if kind == "Az" else (z, yat(step))
        else:
            d, k, off = event[1:]
            k = (0 if d == "D" else k - 1) if sender else k
            step = k if d == "S" else -k
            zz, yy = (zat(off), yat(step)) if kind == "Ay" else (zat(step), yat(off))
        cols = pl.ds(0, QA) if kind[0] == "A" else pl.ds(QA, QB)
        return wbuf.at[c, zz, yy, :, cols]

    def turn(n):
        piece = ob[:, pl.ds(n * Q, Q)].T
        ot[2 * n : 2 * n + 2, :, :, 0:TOK] = piece.reshape(2, 4, RB, TOK)
        part = ot.at[2 * n : 2 * n + 2, :, :, 0:TOK]
        start(remote(part, ot.at[2 * n : 2 * n + 2, :, :, TOK : 2 * TOK], o_send.at[n], o_recv.at[n], sibling))

    turn_at = {4: 0, 10: 1, 18: 2, 26: 3}
    for step, op in enumerate(GATHER):
        for event in op.waits:
            mine = block_of(event, False)
            remote(mine, mine, g_send.at[0], g_recv.at[G_ID[event]], sibling).wait_recv()
        for axis, event in op.sends:
            part = 0 if event[0][0] == "A" else 1
            blk = block_of(event, True)
            remote(blk, blk, g_send.at[part], g_recv.at[G_ID[event]], peer(event, GATHER_TO)).start()
        for event in op.waits:
            part = 0 if event[0][0] == "A" else 1
            mine = block_of(event, False)
            remote(mine, mine, b_send.at[part], b_recv.at[part], sibling).start()
        if step == 0:
            loads[2].wait()
        if step in turn_at:
            turn(turn_at[step])
    for part, gauge in enumerate((gauge_a, gauge_b)):
        remote(gauge, gauge, b_send.at[part], b_recv.at[part], sibling).wait_recv()
    for copy in loads[3:]:
        copy.wait()
    wide = gain_in[...].astype(F32)
    gain_ref[...] = jnp.concatenate([wide[n : n + 1] for n in range(D // 128)], axis=1)

    def forward(m, _):
        rows = pl.ds(pl.multiple_of(m * 320, 320), 320)
        ss = jnp.zeros((320, 1), F32)
        tt = jnp.zeros((320, 1), F32)
        for h in range(2):
            cols = pl.ds(h * H, H)
            w = wbuf[h].reshape(D, H)
            acc = jnp.dot(ob[rows, :], w, preferred_element_type=F32) + xb[rows, cols].astype(F32)
            mixed[h, rows, :] = acc
            eg = eb[rows, cols].astype(F32) * gain_ref[:, cols]
            ss = ss + jnp.sum(acc * acc, axis=1, keepdims=True)
            tt = tt + jnp.sum(acc * eg, axis=1, keepdims=True)
        ss_ref[rows, :] = jnp.broadcast_to(ss, (320, 128))
        t_ref[rows, :] = jnp.broadcast_to(tt, (320, 128))
        return 0

    lax.fori_loop(0, TOK // 320, forward, 0)

    first = (gi * 32 + fi) * 2
    lane = lax.broadcasted_iota(jnp.int32, (8, 128), 1)
    pos = lax.broadcasted_iota(jnp.int32, (SEQ, 128), 0)
    root = 1.0 / math.sqrt(D)
    deltas = []
    for j in range(2):
        rows = pl.ds(j * SEQ, SEQ)
        mask = (pos < len_ref[first + j]).astype(F32)
        scale = lax.rsqrt(ss_ref[rows, :] * (1.0 / D) + EPS)
        t = t_ref[rows, :]
        logp = t * scale * mask * root
        deltas.append(jnp.broadcast_to(jnp.sum(logp, axis=0, keepdims=True), (8, 128)) + off_ref[first + j])
        ss_ref[rows, :] = scale * mask * root
        t_ref[rows, :] = -(scale * scale * scale) * mask * (t * (root / D))
    at = lax.rem(gi, 2) * 64 + 2 * fi
    msg1[...] = jnp.where(lane == at, deltas[0], jnp.where(lane == at + 1, deltas[1], 0.0))

    def prepare(m, _):
        rows = pl.ds(pl.multiple_of(m * 64, 64), 64)
        ga = jnp.concatenate([ss_ref[rows, :]] * 6, axis=1)
        gb = jnp.concatenate([t_ref[rows, :]] * 6, axis=1)
        for h in range(2):
            cols = pl.ds(h * H, H)
            eg = eb[rows, cols].astype(F32) * gain_ref[:, cols]
            mixed[h, rows, :] = ga * eg + gb * mixed[h, rows, :]
        return 0

    for k in range(3):
        start(remote(msg1, my.at[k], y_send.at[k], y_recv.at[k], dev(x, c, z, ys[k])))
    lax.fori_loop(0, 4, prepare, 0)
    total = msg1[...]
    for k in range(3):
        remote(my.at[k], my.at[k], y_send.at[k], y_recv.at[k], sibling).wait_recv()
        total = total + my[k]
    msg2[...] = total
    for k in range(7):
        start(remote(msg2, mz.at[k], z_send.at[k], z_recv.at[k], dev(x, c, zs[k], y)))
    lax.fori_loop(4, 10, prepare, 0)
    for part, gauge in enumerate((gauge_a, gauge_b)):
        remote(gauge, gauge, g_send.at[part], g_recv.at[0], sibling).wait_send()
        remote(gauge, gauge, b_send.at[part], g_recv.at[0], sibling).wait_send()
    for k in range(7):
        remote(mz.at[k], mz.at[k], z_send.at[k], z_recv.at[k], sibling).wait_recv()
        total = total + mz[k]

    prow = jnp.broadcast_to(prow_ref[pl.ds(gi // 2, 1), :], (8, 128))
    for j in range(2):
        base = jnp.sum(jnp.where(prow == pid_ref[first + j], total, 0.0), axis=1, keepdims=True) * (1.0 / SAMPLES)
        crow[j] = deltas[j] - base

    def gradient(m, _):
        rows = pl.ds(pl.multiple_of(m * 64, 64), 64)
        cc = jnp.where(m < 5, crow[0], crow[1])[0:1]
        cc = jnp.concatenate([cc] * 6, axis=1)
        for h in range(2):
            value = (mixed[h, rows, :] * cc).astype(BF16)
            g[h, rows, :] = value
            rg_out[rows, h * H : (h + 1) * H] = value
        gall[rows, :] = g[c, rows, :]
        return 0

    lax.fori_loop(0, TOK // 64, gradient, 0)
    pieces = (pl.ds(0, QA), pl.ds(QA, QB))
    for n, cols in enumerate(pieces):
        theirs = gall.at[pl.ds(TOK, TOK), cols]
        start(remote(g.at[1 - c, :, cols], theirs, h_send.at[n], h_recv.at[n], sibling))
    for n in range(4):
        theirs = ot.at[2 * n : 2 * n + 2, :, :, TOK : 2 * TOK]
        remote(theirs, theirs, o_send.at[n], o_recv.at[n], sibling).wait_recv()
    taken = set()

    def take(n):
        if n not in taken:
            taken.add(n)
            theirs = gall.at[pl.ds(TOK, TOK), pieces[n]]
            remote(theirs, theirs, h_send.at[n], h_recv.at[n], sibling).wait_recv()

    def slot(event):
        kind, d = event[:2]
        if kind == "Ay":
            n = (0 if d == "L" else 2) + event[2] - 1
            return sa.at[n, event[3]], ra.at[n, event[3]], a_send
        if kind == "Az":
            n = list(SCATTER_TO).index(d)
            return sa2.at[n], ra2.at[n], a2_send
        if kind == "Bz":
            n = (0 if d == "L" else 4) + event[2] - 1
            return sb.at[n, event[3]], rb.at[n, event[3]], s_send
        n = (2, -1, 1).index(d)
        return sb2.at[n], rb2.at[n], s2_send

    def push(event, value):
        src, dst, sem = slot(event)
        src[...] = value.astype(BF16)
        remote(src, dst, sem.at[0], r_recv.at[S_ID[event]], peer(event, SCATTER_TO)).start()

    xr, xg = (xra, xrb), (xga, xgb)

    def got_of(event):
        if event[0] == "X":
            return xr[event[1]].at[lax.rem(x + NX - 1 - event[2], NX)]
        if event[0] == "G":
            return xg[event[1]].at[1 - c]
        if event[0] == "l1":
            return ls
        if event[0] == "l2":
            return lx.at[lax.rem(x + NX - 1 - event[1], NX)]
        return slot(event)[1]

    def spread(ab, value):
        xr[ab][x] = value.astype(BF16)
        for k in range(3):
            blk = xr[ab].at[x]
            remote(blk, blk, x_send.at[ab], r_recv.at[S_ID["X", ab, k]], dev(xs[k], c, z, y)).start()

    for op in SCATTER:
        got = 0.0
        for event in op.waits:
            dst = got_of(event)
            remote(dst, dst, a_send.at[0], r_recv.at[S_ID[event]], sibling).wait_recv()
            if event[0] in ("Ay", "Az", "By", "Bz"):
                got = got + dst[...].astype(F32)
        kind = op.key[0] if isinstance(op.key, tuple) else op.key
        if kind == "CA":
            take(0)
            yy = yat(Y_LEAVE[op.key[1]])
            lhs = ot[:, yy].reshape(8 * RB, 2 * TOK)
            da[:, yy] = jnp.dot(lhs, gall[:, 0:QA], preferred_element_type=F32).reshape(8, RB, QA)
            for axis, event in op.sends:
                push(event, da[zat(Z_LEAVE[event[3]]), yy])
        elif kind == "CB":
            take(1)
            zz = zat(Z_LEAVE[op.key[1]])
            lhs = ot[zz].reshape(4 * RB, 2 * TOK)
            db[zz] = jnp.dot(lhs, gall[:, QA:H], preferred_element_type=F32).reshape(4, RB, QB)
            for axis, event in op.sends:
                push(event, db[zz, yat(Y_LEAVE[event[3]])])
        elif kind == "FA":
            push(op.sends[0][1], da[zat(Z_LEAVE[op.key[1]]), yat(1)] + got)
            push(op.sends[1][1], da[zat(Z_LEAVE[op.key[1]]), yat(-1)])
        elif kind == "TA":
            value = da[zat(Z_LEAVE[op.key[1]]), y] + got
            if Z_LEAVE[op.key[1]]:
                push(op.sends[0][1], value)
            else:
                spread(0, value)
        elif kind == "FB":
            value = db[zat(Z_LEAVE[op.key[1]]), yat(Y_LEAVE[op.key[2]])] + got
            if op.sends[0][0] != "x":
                push(op.sends[0][1], value)
            else:
                spread(1, value)
        elif kind == "X":
            ab = op.key[1]
            part = [xr[ab][n].astype(F32) for n in range(NX)]
            value = ((part[0] + part[1]) + (part[2] + part[3])) * (1.0 / 512.0)
            xg[ab][c] = value
            blk = xg[ab].at[c]
            start(remote(blk, blk, q_send.at[ab], r_recv.at[S_ID["G", ab]], sibling))
        elif kind == "W":
            ab = op.key[1]
            for h in range(2):
                wg_ref[:, pl.ds(h * H + ab * QA, (QA, QB)[ab])] = xg[ab][h]
        elif kind == "pair":
            pair = lmsg1[...] + ls[...]
            lmsg2[...] = pair
            lx[x] = pair
            for k in range(3):
                start(remote(lmsg2, lx.at[x], m_send.at[k], r_recv.at[S_ID["l2", k]], dev(xs[k], c, z, y)))
        elif kind == "total":
            whole = (lx[0] + lx[1]) + (lx[2] + lx[3])
            loss_ref[0, 0] = jnp.sum(whole[0:1, 0:1]) * (1.0 / (512 * SEQ))
        elif kind == "attn":
            n = op.key[1]
            cols = pl.ds(n * Q, Q)
            w0 = wbuf[0, 2 * n : 2 * n + 2].reshape(Q, H)
            w1 = wbuf[1, 2 * n : 2 * n + 2].reshape(Q, H)
            dims = (((1,), (1,)), ((), ()))
            acc = lax.dot_general(g[0], w0, dims, preferred_element_type=F32)
            acc = acc + lax.dot_general(g[1], w1, dims, preferred_element_type=F32)
            ag_out[:, cols] = acc.astype(BF16)
        else:
            square = jnp.zeros((8, 1), F32)
            for p in range(PPG):
                member = prow == gi * PPG + p
                base = jnp.sum(jnp.where(member, total, 0.0), axis=1, keepdims=True) * (1.0 / SAMPLES)
                off = jnp.where(member, total - base, 0.0)
                square = square + jnp.sum(off * off, axis=1, keepdims=True)
            lmsg1[...] = jnp.broadcast_to(square, (8, 128))
            start(remote(lmsg1, ls, l_send.at[0], r_recv.at[S_ID[("l1",)]], sibling))

    for ref, sem in ((sa, a_send), (sa2, a2_send), (sb, s_send), (sb2, s2_send)):
        remote(ref, ref, sem.at[0], r_recv.at[0], sibling).wait_send()
    for ab in range(2):
        ref = xr[ab].at[0:3]
        remote(ref, ref, x_send.at[ab], r_recv.at[0], sibling).wait_send()
    for copy in sent:
        copy.wait_send()


def local(
    resid_in, attn_out, target_rows, out_weight, norm_gain,
    seq_lengths, prompt_ids, log_offsets, plan_dest, plan_slot,
):
    hbm = pl.BlockSpec(memory_space=pl.ANY)
    vmem = pl.BlockSpec(memory_space=pltpu.VMEM)
    smem = pl.BlockSpec(memory_space=pltpu.SMEM)
    dma = pltpu.SemaphoreType.DMA
    n_g, n_s = len(G_ID), len(S_ID)
    scratch = [
        pltpu.VMEM((2, NZ, NY, RB, H), BF16),
        pltpu.VMEM((TOK, D), BF16),
        pltpu.VMEM((TOK, D), BF16),
        pltpu.VMEM((TOK, D), BF16),
        pltpu.VMEM((NZ, NY, RB, 2 * TOK), BF16),
        pltpu.VMEM((2, TOK, H), F32),
        pltpu.VMEM((TOK, 128), F32),
        pltpu.VMEM((TOK, 128), F32),
        pltpu.VMEM((2, TOK, H), BF16),
        pltpu.VMEM((2 * TOK, H), BF16),
        pltpu.VMEM((NZ, NY, RB, QA), F32),
        pltpu.VMEM((NZ, NY, RB, QB), F32),
        pltpu.VMEM((3, 8, RB, QA), BF16),
        pltpu.VMEM((3, 8, RB, QA), BF16),
        pltpu.VMEM((7, RB, QA), BF16),
        pltpu.VMEM((7, RB, QA), BF16),
        pltpu.VMEM((7, 4, RB, QB), BF16),
        pltpu.VMEM((7, 4, RB, QB), BF16),
        pltpu.VMEM((3, RB, QB), BF16),
        pltpu.VMEM((3, RB, QB), BF16),
        pltpu.VMEM((4, RB, QA), BF16),
        pltpu.VMEM((4, RB, QB), BF16),
        pltpu.VMEM((2, RB, QA), F32),
        pltpu.VMEM((2, RB, QB), F32),
        pltpu.VMEM((3, 8, 128), F32),
        pltpu.VMEM((7, 8, 128), F32),
        pltpu.VMEM((8, 128), F32),
        pltpu.VMEM((8, 128), F32),
        pltpu.VMEM((8, 128), F32),
        pltpu.VMEM((4, 8, 128), F32),
        pltpu.VMEM((8, 128), F32),
        pltpu.VMEM((8, 128), F32),
        pltpu.VMEM((2, 8, 128), F32),
        pltpu.VMEM((D // 128, 128), BF16),
        pltpu.VMEM((1, D), F32),
        pltpu.SMEM((512,), jnp.int32),
        pltpu.SMEM((512,), jnp.int32),
        pltpu.SMEM((512,), F32),
        pltpu.VMEM((4, 128), jnp.int32),
        pltpu.VMEM((31, RB, QA), BF16),
        pltpu.VMEM((31, RB, QB), BF16),
        dma((10,)),
        dma((2,)), dma((n_g,)), dma((2,)), dma((2,)),
        dma((4,)), dma((4,)), dma((2,)), dma((2,)),
        dma((n_s,)),
        dma((1,)), dma((1,)), dma((1,)), dma((1,)), dma((2,)), dma((2,)),
        dma((3,)), dma((3,)), dma((7,)), dma((7,)),
        dma((1,)), dma((3,)),
    ]
    call = pl.pallas_call(
        kernel,
        out_shape=(
            pltpu.VMEM((TOK, D), BF16),
            pltpu.VMEM((TOK, D), BF16),
            pltpu.VMEM((RB, D), F32),
            jax.ShapeDtypeStruct((1, 1), F32),
        ),
        in_specs=[hbm] * 9,
        out_specs=(vmem, vmem, vmem, smem),
        scratch_shapes=scratch,
        name="balance",
        compiler_params=pltpu.CompilerParams(
            collective_id=0, has_side_effects=True, vmem_limit_bytes=48 * 1024 * 1024
        ),
        cost_estimate=pl.CostEstimate(flops=9060000000, bytes_accessed=10000000, transcendentals=640),
    )
    operands = (
        resid_in.reshape(TOK, D),
        attn_out.reshape(TOK, D),
        target_rows.reshape(TOK, D),
        out_weight,
        norm_gain.reshape(D // 128, 128),
        seq_lengths,
        prompt_ids,
        log_offsets,
        prompt_ids.reshape(4, 128),
    )
    rg, ag, wg, loss = call(*(pltpu.with_memory_space_constraint(v, pltpu.HBM) for v in operands))
    return rg.reshape(2, SEQ, D), ag.reshape(2, SEQ, D), wg, loss.reshape(())


def solution(mesh):
    return jax.shard_map(
        local,
        mesh=mesh,
        in_specs=(
            P(("group", "fsdp"), None, None),
            P(("group", "fsdp"), None, None),
            P(("group", "fsdp"), None, None),
            P("fsdp", None),
            P(), P(), P(), P(), P(), P(),
        ),
        out_specs=(
            P(("group", "fsdp"), None, None),
            P(("group", "fsdp"), None, None),
            P("fsdp", None),
            P(),
        ),
        check_vma=False,
    )
```
